32 devices in a mesh: grp: 2 (over y), seq: 4 (over z), sub: 2 (over x), hd: 2 (over core).
Axes of the slice: x: 2, y: 2, z: 4, core: 2. Of those that a mesh axis runs over, the one named last changes fastest.
Arguments:
- queries: bfloat16 [8192, 768], P(('grp', 'seq', 'sub'), 'hd'), parts along dimension 0, may hold values from -200 to 200
- keys: bfloat16 [8192, 768], P(('grp', 'seq', 'sub'), 'hd'), parts along dimension 0, may hold values from -10 to 10
- values: bfloat16 [8192, 768], P(('grp', 'seq', 'sub'), 'hd'), parts along dimension 0, may hold values from -6 to 6
- grad_out: bfloat16 [8192, 768], P(('grp', 'seq', 'sub'), 'hd'), parts along dimension 0, may hold values from -6 to 6
- center_head_shift: int32 [16], replicated, may hold values from 0 to 7
- wide_head_shift: int32 [16], replicated, may hold values from 0 to 127
- valid_count: int32 [2], P('grp'), parts along dimension 0, may hold values from 2048 to 4096
Outputs:
- attended: bfloat16 [8192, 768], P(('grp', 'seq', 'sub'), 'hd'), parts along dimension 0
- grad_queries: bfloat16 [8192, 768], P(('grp', 'seq', 'sub'), 'hd'), parts along dimension 0
- key_gradient: bfloat16 [8192, 768], P(('grp', 'seq', 'sub'), 'hd'), parts along dimension 0
- value_gradient: bfloat16 [8192, 768], P(('grp', 'seq', 'sub'), 'hd'), parts along dimension 0
The draws below stay inside these ranges and needn't reach their ends.
There are 2 independent parts, one for each index of `grp`. The reference program is written for one: setup_inputs(seed, part) draws one part's arguments, and reference() takes and returns one part's arrays. A program takes and returns all parts, laid end to end along the dimension named above; an argument that names none is the same for every part. Nothing has to cross between parts.
All inputs are finite; a program needn't handle non-finite values.
Results may differ from the reference program's by a relative error of at most 0.0095.
Values may be sent and summed in bfloat16 or wider, within the bound.
No kernel may reach another device: no remote copies, remote signals or barrier semaphores. Data moves between devices by JAX's collectives and lax.ppermute only.
A program may use at most 64 MiB of HBM per device.

```python
import jax
import jax.numpy as jnp
from jax import lax

HEAD_COUNT = 16
HEAD_WIDTH = 48
MODEL_WIDTH = 768
CENTER_DILATION = 8
WIDE_DILATION = 128
LOCAL = 512
CENTER_LENGTH = 1024
SLIDE_TOKENS = 4096


def draw_queries(key, part):
    key = jax.random.fold_in(key, 1)
    base_key = jax.random.fold_in(key, 0)
    base = jnp.clip(2.0 * jax.random.normal(base_key, (SLIDE_TOKENS, MODEL_WIDTH), jnp.float32), -10.0, 10.0)
    return base.astype(jnp.bfloat16)


def draw_keys(key, part):
    key = jax.random.fold_in(key, 2)
    base_key = jax.random.fold_in(key, 0)
    base = jnp.clip(jax.random.normal(base_key, (SLIDE_TOKENS, MODEL_WIDTH), jnp.float32), -5.0, 5.0)
    return base.astype(jnp.bfloat16)


def plant(values, own_key, low, top_value):
    extent = values.shape
    spot = [jax.random.randint(jax.random.fold_in(own_key, axis), (), 0, extent[axis]) for axis in range(len(extent))]
    values = values.at[tuple(spot)].set(low)
    longest = extent.index(max(extent))
    spot[longest] = (spot[longest] + 1) % extent[longest]
    return values.at[tuple(spot)].set(top_value)


def steps_of(stream_key, dims, cuts, low, largest):
    gain, own = 1.0, jax.random.fold_in(stream_key, 6)
    for axis_at, blocks in cuts:
        steps = jnp.exp(jax.random.uniform(jax.random.fold_in(own, axis_at), (blocks,), jnp.float32, low / len(cuts), largest / len(cuts)))
        gain = gain * jnp.repeat(steps, dims[axis_at] // blocks).reshape([-1 if axis == axis_at else 1 for axis in range(len(dims))])
    return gain


def centred(key, extent, width, most, shards=(), held_as=jnp.bfloat16):
    values = width * jax.random.normal(key, extent, jnp.float32)
    if shards:
        values = values * steps_of(key, extent, shards, -0.22, 0.18)
    return jnp.clip(values, -most, most).astype(held_as)


def setup_inputs(seed: int = 0, part: int = 0) -> dict:
    seeds = jax.random.split(jax.random.key(seed), 8)
    own_keys = jax.random.split(jax.random.fold_in(seeds[7], part), 8)
    queries = draw_queries(jax.random.fold_in(jax.random.fold_in(seeds[7], part), 71), part)
    keys = draw_keys(jax.random.fold_in(jax.random.fold_in(seeds[7], part), 71), part)
    values = centred(own_keys[2], (SLIDE_TOKENS, MODEL_WIDTH), 1.0, 6.0, ((0, 8), (1, 2)))
    grad_out = centred(own_keys[3], (SLIDE_TOKENS, MODEL_WIDTH), 1.0, 6.0, ((0, 8), (1, 2)))
    center_head_shift = plant(jax.random.randint(seeds[4], (HEAD_COUNT,), 0, CENTER_DILATION), jax.random.fold_in(seeds[4], 1), 0, CENTER_DILATION - 1).astype(jnp.int32)
    wide_head_shift = plant(jax.random.randint(seeds[5], (HEAD_COUNT,), 0, WIDE_DILATION), jax.random.fold_in(seeds[5], 1), 0, WIDE_DILATION - 1).astype(jnp.int32)
    valid_count = jax.random.randint(own_keys[6], (1,), SLIDE_TOKENS // 2, SLIDE_TOKENS + 1).astype(jnp.int32)
    return dict(queries=queries, keys=keys, values=values, grad_out=grad_out, center_head_shift=center_head_shift, wide_head_shift=wide_head_shift, valid_count=valid_count)


def head_pass(queries_h, key_rows, value_rows, live_mask, grad_rows):
    scaling = HEAD_WIDTH ** -0.5
    query_wide = queries_h.astype(jnp.float32)
    key_wide = key_rows.astype(jnp.float32)
    value_wide = value_rows.astype(jnp.float32)
    grad_wide = grad_rows.astype(jnp.float32)
    scores = scaling * jnp.dot(query_wide, key_wide.T)
    scores = jnp.where(live_mask[None, :], scores, -1e30)
    row_max = jnp.max(scores, axis=1, keepdims=True)
    lifted = jnp.where(live_mask[None, :], jnp.exp(scores - row_max), 0.0)
    attn_prob = lifted / jnp.sum(lifted, axis=1, keepdims=True)
    weights = attn_prob.astype(jnp.bfloat16)
    weights_wide = weights.astype(jnp.float32)
    context = jnp.dot(weights_wide, value_wide)
    delta_row = jnp.sum(grad_wide * context, axis=1, keepdims=True)
    grad_prob = jnp.dot(grad_wide, value_wide.T)
    dscore = (scaling * attn_prob * (grad_prob - delta_row)).astype(jnp.bfloat16)
    dscore_wide = dscore.astype(jnp.float32)
    grad_query = jnp.dot(dscore_wide, key_wide).astype(jnp.bfloat16)
    grad_key = jnp.dot(dscore_wide.T, query_wide)
    grad_value = jnp.dot(weights_wide.T, grad_wide)
    return context.astype(jnp.bfloat16), grad_query, grad_key, grad_value


def select_row_set(source, step, offsets):
    shaped = source.reshape(source.shape[0] // step, step, HEAD_COUNT, HEAD_WIDTH)
    picker = (jnp.arange(step, dtype=jnp.int32)[:, None] == offsets[None, :].astype(jnp.int32))
    return jnp.sum(jnp.where(picker[None, :, :, None], shaped, jnp.zeros((), source.dtype)), axis=1).astype(source.dtype)


def distribute_row_set(rows, step, offsets):
    picker = (jnp.arange(step, dtype=jnp.int32)[:, None] == offsets[None, :].astype(jnp.int32))
    spread = jnp.where(picker[None, :, :, None], rows[:, None, :, :], jnp.zeros((), rows.dtype))
    return spread.reshape(rows.shape[0] * step, HEAD_COUNT * HEAD_WIDTH)


def reference(queries, keys, values, grad_out, center_head_shift, wide_head_shift, valid_count):
    valid_len = valid_count[0].astype(jnp.int32)
    heads_q = queries.reshape(SLIDE_TOKENS, HEAD_COUNT, HEAD_WIDTH)
    heads_k = keys.reshape(SLIDE_TOKENS, HEAD_COUNT, HEAD_WIDTH)
    heads_v = values.reshape(SLIDE_TOKENS, HEAD_COUNT, HEAD_WIDTH)
    heads_g = grad_out.reshape(SLIDE_TOKENS, HEAD_COUNT, HEAD_WIDTH)
    center_key_rows = select_row_set(keys, CENTER_DILATION, center_head_shift)
    center_value_rows = select_row_set(values, CENTER_DILATION, center_head_shift)
    wide_key_rows = select_row_set(keys, WIDE_DILATION, wide_head_shift)
    wide_value_rows = select_row_set(values, WIDE_DILATION, wide_head_shift)
    center_piece_rows = CENTER_LENGTH // CENTER_DILATION
    wide_token_count = SLIDE_TOKENS // WIDE_DILATION
    wide_places = (jnp.arange(wide_token_count, dtype=jnp.int32)[:, None] * WIDE_DILATION + wide_head_shift[None, :].astype(jnp.int32)).astype(jnp.int32)
    far_live = wide_places < valid_len
    mapped = jax.vmap(head_pass, in_axes=(1, 1, 1, 1, 1), out_axes=(1, 1, 1, 1))

    def segment(carry, index):
        mid_acc_k, mid_acc_v, far_acc_k, far_acc_v = carry
        begin = (index * LOCAL).astype(jnp.int32)
        center_index = (begin // CENTER_LENGTH).astype(jnp.int32)
        mid_begin = (center_index * center_piece_rows).astype(jnp.int32)
        seg_q = lax.dynamic_slice_in_dim(heads_q, begin, LOCAL, 0)
        seg_k = lax.dynamic_slice_in_dim(heads_k, begin, LOCAL, 0)
        seg_v = lax.dynamic_slice_in_dim(heads_v, begin, LOCAL, 0)
        seg_g = lax.dynamic_slice_in_dim(heads_g, begin, LOCAL, 0)
        seg_mid_k = lax.dynamic_slice_in_dim(center_key_rows, mid_begin, center_piece_rows, 0)
        seg_mid_v = lax.dynamic_slice_in_dim(center_value_rows, mid_begin, center_piece_rows, 0)
        local_pos = begin + jnp.arange(LOCAL, dtype=jnp.int32)
        local_live = jnp.broadcast_to((local_pos < valid_len)[:, None], (LOCAL, HEAD_COUNT))
        center_places = (center_index * CENTER_LENGTH + jnp.arange(center_piece_rows, dtype=jnp.int32)[:, None] * CENTER_DILATION + center_head_shift[None, :].astype(jnp.int32)).astype(jnp.int32)
        live_all = jnp.concatenate([local_live, center_places < valid_len, far_live], axis=0)
        key_all = jnp.concatenate([seg_k, seg_mid_k, wide_key_rows], axis=0)
        value_all = jnp.concatenate([seg_v, seg_mid_v, wide_value_rows], axis=0)
        out_seg, dq_seg, dk_all, dv_all = mapped(seg_q, key_all, value_all, live_all, seg_g)
        upper = LOCAL + center_piece_rows
        old_k = lax.dynamic_slice_in_dim(mid_acc_k, mid_begin, center_piece_rows, 0)
        old_v = lax.dynamic_slice_in_dim(mid_acc_v, mid_begin, center_piece_rows, 0)
        mid_acc_k = lax.dynamic_update_slice_in_dim(mid_acc_k, old_k + dk_all[LOCAL:upper], mid_begin, 0)
        mid_acc_v = lax.dynamic_update_slice_in_dim(mid_acc_v, old_v + dv_all[LOCAL:upper], mid_begin, 0)
        far_acc_k = far_acc_k + dk_all[upper:]
        far_acc_v = far_acc_v + dv_all[upper:]
        return (mid_acc_k, mid_acc_v, far_acc_k, far_acc_v), (out_seg, dq_seg, dk_all[:LOCAL], dv_all[:LOCAL])

    opening_totals = (jnp.zeros((SLIDE_TOKENS // CENTER_DILATION, HEAD_COUNT, HEAD_WIDTH), jnp.float32), jnp.zeros((SLIDE_TOKENS // CENTER_DILATION, HEAD_COUNT, HEAD_WIDTH), jnp.float32),
                 jnp.zeros((wide_token_count, HEAD_COUNT, HEAD_WIDTH), jnp.float32), jnp.zeros((wide_token_count, HEAD_COUNT, HEAD_WIDTH), jnp.float32))
    closing_totals, piled_arrays = lax.scan(segment, opening_totals, jnp.arange(SLIDE_TOKENS // LOCAL, dtype=jnp.int32))
    attended = piled_arrays[0].reshape(SLIDE_TOKENS, MODEL_WIDTH)
    grad_queries = piled_arrays[1].reshape(SLIDE_TOKENS, MODEL_WIDTH)
    key_gradient = piled_arrays[2].reshape(SLIDE_TOKENS, MODEL_WIDTH) + distribute_row_set(closing_totals[0], CENTER_DILATION, center_head_shift) + distribute_row_set(closing_totals[2], WIDE_DILATION, wide_head_shift)
    value_gradient = piled_arrays[3].reshape(SLIDE_TOKENS, MODEL_WIDTH) + distribute_row_set(closing_totals[1], CENTER_DILATION, center_head_shift) + distribute_row_set(closing_totals[3], WIDE_DILATION, wide_head_shift)
    return attended, grad_queries, key_gradient.astype(jnp.bfloat16), value_gradient.astype(jnp.bfloat16)
```

```python
import functools
import math

import jax
import jax.numpy as jnp
from jax import lax
from jax.experimental import pallas as pl
from jax.experimental.pallas import tpu as pltpu
from jax.sharding import PartitionSpec as P

HEAD_WIDTH = 48
CENTER_DILATION = 8
WIDE_DILATION = 128
LANES = 128
DEAD = -1e30
SCALE = HEAD_WIDTH**-0.5
EXP2_SCALE = SCALE * math.log2(math.e)
F32 = jnp.float32
BF16 = jnp.bfloat16

VMEM = pl.BlockSpec(memory_space=pltpu.VMEM)
SMEM = pl.BlockSpec(memory_space=pltpu.SMEM)


def nn(a, b):
    return jnp.dot(a, b, preferred_element_type=F32)


def nt(a, b):
    return lax.dot_general(a, b, (((1,), (1,)), ((), ())), preferred_element_type=F32)


def head_rows(h):
    return slice(h * HEAD_WIDTH, (h + 1) * HEAD_WIDTH)


def window(h):
    low = h * HEAD_WIDTH // LANES * LANES
    high = -(-(h + 1) * HEAD_WIDTH // LANES) * LANES
    return low, high


def embed(rows, h):
    low, high = window(h)
    before, after = h * HEAD_WIDTH - low, high - (h + 1) * HEAD_WIDTH
    parts = [rows]
    if before:
        parts.insert(0, jnp.zeros((before, rows.shape[1]), rows.dtype))
    if after:
        parts.append(jnp.zeros((after, rows.shape[1]), rows.dtype))
    return jnp.concatenate(parts, axis=0) if len(parts) > 1 else rows


def add_window(ref, rows, h, value, started):
    low, high = window(h)
    for at in range(low, high, LANES):
        part = value[:, at - low : at - low + LANES]
        if at in started:
            ref[rows, at : at + LANES] += part
        else:
            started.add(at)
            ref[rows, at : at + LANES] = part


def lane_shifts(shift_ref, base, heads, width):
    lane = lax.broadcasted_iota(jnp.int32, (1, width), 1)
    row = jnp.zeros((1, width), jnp.int32)
    for h in range(heads):
        inside = (lane >= h * HEAD_WIDTH) & (lane < (h + 1) * HEAD_WIDTH)
        row = jnp.where(inside, shift_ref[base + h], row)
    return row


def select_kernel(heads, base_ref, center_ref, wide_ref, k_ref, v_ref, near_ref, far_ref, wide_f32):
    rows, width = k_ref.shape
    base = base_ref[0]
    center = lane_shifts(center_ref, base, heads, width)
    wide = lane_shifts(wide_ref, base, heads, width)
    near_rows = rows // CENTER_DILATION
    far_rows = rows // WIDE_DILATION
    row = lax.broadcasted_iota(jnp.int32, (far_rows, WIDE_DILATION, LANES), 1)
    for at, ref in ((0, k_ref), (width, v_ref)):
        for low in range(0, width, LANES):
            lanes = slice(low, low + LANES)
            spread = ref[:, lanes].astype(F32)
            wide_f32[...] = spread
            picked = jnp.zeros((near_rows, LANES), F32)
            for step in range(CENTER_DILATION):
                rows_at = wide_f32[pl.ds(step, near_rows, stride=CENTER_DILATION), :]
                picked = jnp.where(center[:, lanes] == step, rows_at, picked)
            near_ref[:, at + low : at + low + LANES] = picked.astype(BF16)
            chosen = jnp.where(row == wide[:, lanes], spread.reshape(far_rows, WIDE_DILATION, LANES), 0.0)
            far_ref[:, at + low : at + low + LANES] = jnp.sum(chosen, axis=1).astype(BF16)


def forward_kernel(
    heads, live_ref, q_ref, k_ref, v_ref, g_ref,
    p_ref, qt_ref, gt_ref, kt_ref, ot_ref, max_ref, sum_ref, vt_ref,
):
    rows = q_ref.shape[0]
    qt_ref[...] = q_ref[...].T
    gt_ref[...] = g_ref[...].T
    kt_ref[...] = k_ref[...].T
    vt_ref[...] = v_ref[...].T
    live = lax.broadcasted_iota(jnp.int32, (rows, rows), 0) < live_ref[0]
    for h in range(heads):
        low, high = window(h)
        scores = nn(k_ref[:, low:high], embed(qt_ref[head_rows(h), :], h))
        scores = jnp.where(live, scores, DEAD)
        top = jnp.max(scores, axis=0, keepdims=True)
        lifted = jnp.exp2((scores - top) * EXP2_SCALE)
        max_ref[h : h + 1, :] = top
        sum_ref[h : h + 1, :] = jnp.sum(lifted, axis=0, keepdims=True)
        weights = lifted.astype(BF16)
        p_ref[h] = weights
        ot_ref[head_rows(h), :] = nn(vt_ref[head_rows(h), :], weights)


def remote_kernel(
    heads, base_ref, center_ref, wide_ref, valid_ref,
    place_ref, near_ref, came_ref, far_ref, qt_ref, gt_ref, o1_ref, max_ref, sum_ref,
    out_ref, factor_ref, delta_ref, dq_ref, own_ref, send_ref, wides_ref,
    kr_ref, vr_ref, krt_ref, vrt_ref, ot_ref, dk_ref, dv_ref,
):
    width, rows = qt_ref.shape
    near_rows = near_ref.shape[0]
    far_rows = far_ref.shape[0]
    count = 2 * near_rows + far_rows
    base = base_ref[0]
    for at, ref, turned in ((0, kr_ref, krt_ref), (width, vr_ref, vrt_ref)):
        ref[:near_rows, :] = near_ref[:, at : at + width]
        ref[near_rows : 2 * near_rows, :] = came_ref[:, at : at + width]
        ref[2 * near_rows :, :] = far_ref[:, at : at + width]
        turned[...] = ref[...].T
    place = jnp.broadcast_to(place_ref[:, 0:1], (count, rows))
    is_near = lax.broadcasted_iota(jnp.int32, (count, rows), 0) < 2 * near_rows
    began_k, began_v = set(), set()
    everything = slice(0, count)
    for h in range(heads):
        low, high = window(h)
        q_rows = embed(qt_ref[head_rows(h), :], h)
        g_head = gt_ref[head_rows(h), :]
        g_rows = embed(g_head, h)
        scores = nn(kr_ref[:, low:high], q_rows)
        limit = jnp.where(
            is_near, valid_ref[0] - center_ref[base + h], valid_ref[0] - wide_ref[base + h]
        )
        scores = jnp.where(place < limit, scores, DEAD)
        top_here = max_ref[h : h + 1, :]
        top = jnp.maximum(jnp.max(scores, axis=0, keepdims=True), top_here)
        lifted = jnp.exp2((scores - top) * EXP2_SCALE)
        keep = jnp.exp2((top_here - top) * EXP2_SCALE)
        total = sum_ref[h : h + 1, :] * keep + jnp.sum(lifted, axis=0, keepdims=True)
        inverse = 1.0 / total
        prob = lifted * inverse
        factor = keep * inverse
        weights = prob.astype(BF16)
        context = o1_ref[head_rows(h), :] * factor + nn(vrt_ref[head_rows(h), :], weights)
        ot_ref[head_rows(h), :] = context
        delta = jnp.sum(g_head.astype(F32) * context, axis=0, keepdims=True)
        factor_ref[h : h + 1, :] = factor
        delta_ref[h : h + 1, :] = delta
        grad_prob = nn(vr_ref[:, low:high], g_rows)
        dscore = (prob * (grad_prob - delta)).astype(BF16)
        dq_ref[head_rows(h), :] = nn(krt_ref[head_rows(h), :], dscore)
        add_window(dk_ref, everything, h, nt(dscore, q_rows), began_k)
        add_window(dv_ref, everything, h, nt(weights, g_rows), began_v)
    out_ref[...] = ot_ref[...].astype(BF16).T
    for at, ref, by in ((0, dk_ref, SCALE), (width, dv_ref, None)):
        value = ref[...] * by if by is not None else ref[...]
        own_ref[:, at : at + width] = value[:near_rows].astype(own_ref.dtype)
        send_ref[:, at : at + width] = value[near_rows : 2 * near_rows].astype(send_ref.dtype)
        wides_ref[:, at : at + width] = value[2 * near_rows :].astype(wides_ref.dtype)


def backward_kernel(
    heads, p_ref, qt_ref, gt_ref, kt_ref, k_ref, v_ref, factor_ref, delta_ref, dq2_ref,
    dq_ref, dk_ref, dv_ref, dqt_ref,
):
    rows = k_ref.shape[0]
    began_k, began_v = set(), set()
    everything = slice(0, rows)
    for h in range(heads):
        low, high = window(h)
        q_rows = embed(qt_ref[head_rows(h), :], h)
        g_rows = embed(gt_ref[head_rows(h), :], h)
        prob = p_ref[h].astype(F32) * factor_ref[h : h + 1, :]
        grad_prob = nn(v_ref[:, low:high], g_rows)
        dscore = (prob * (grad_prob - delta_ref[h : h + 1, :])).astype(BF16)
        dqt_ref[head_rows(h), :] = dq2_ref[head_rows(h), :] + nn(kt_ref[head_rows(h), :], dscore)
        add_window(dk_ref, everything, h, nt(dscore, q_rows), began_k)
        add_window(dv_ref, everything, h, nt(prob.astype(BF16), g_rows), began_v)
    dq_ref[...] = (dqt_ref[...] * SCALE).astype(BF16).T
    dk_ref[...] = dk_ref[...] * SCALE


def combine_kernel(
    heads, base_ref, center_ref, wide_ref, dk_ref, dv_ref, own_ref, came_ref, far_ref,
    outk_ref, outv_ref, sum_ref,
):
    rows, width = dk_ref.shape
    base = base_ref[0]
    center = lane_shifts(center_ref, base, heads, width)
    wide = lane_shifts(wide_ref, base, heads, width)
    near_rows = own_ref.shape[0]
    far_rows = far_ref.shape[0]
    row = lax.broadcasted_iota(jnp.int32, (WIDE_DILATION, LANES), 0)
    for at, ref, out in ((0, dk_ref, outk_ref), (width, dv_ref, outv_ref)):
        for low in range(0, width, LANES):
            lanes = slice(low, low + LANES)
            packed = slice(at + low, at + low + LANES)
            near = own_ref[:, packed].astype(F32) + came_ref[:, packed].astype(F32)
            for block in range(far_rows):
                part = slice(block * WIDE_DILATION, (block + 1) * WIDE_DILATION)
                far = far_ref[block : block + 1, packed].astype(F32)
                sum_ref[part, :] = ref[part, lanes] + jnp.where(row == wide[:, lanes], far, 0.0)
            for step in range(CENTER_DILATION):
                strided = pl.ds(step, near_rows, stride=CENTER_DILATION)
                sum_ref[strided, :] += jnp.where(center[:, lanes] == step, near, 0.0)
            out[:, lanes] = sum_ref[...].astype(BF16)


def call(body, outs, ins, scratch=(), flops=0, moved=0):
    return pl.pallas_call(
        body,
        out_shape=[jax.ShapeDtypeStruct(s, d) for s, d in outs],
        in_specs=[SMEM if scalar else VMEM for scalar in ins],
        out_specs=[VMEM] * len(outs),
        scratch_shapes=[pltpu.VMEM(s, d) for s, d in scratch],
        compiler_params=pltpu.CompilerParams(vmem_limit_bytes=48 * 2**20),
        cost_estimate=pl.CostEstimate(flops=flops, bytes_accessed=moved, transcendentals=0),
    )


def local(queries, keys, values, grad_out, center_shift, wide_shift, valid_count):
    rows, width = queries.shape
    heads = width // HEAD_WIDTH
    near_rows, far_own = rows // CENTER_DILATION, rows // WIDE_DILATION
    axes = ("seq", "sub")
    devices = lax.axis_size(axes)
    device = lax.axis_index(axes)
    base = (lax.axis_index("hd") * heads).astype(jnp.int32).reshape(1)
    far_rows = far_own * devices
    count = 2 * near_rows + far_rows

    def swap(value, apart):
        return lax.ppermute(value, axes, [(at, at ^ apart) for at in range(devices)])

    near, far = call(
        functools.partial(select_kernel, heads),
        [((near_rows, 2 * width), BF16), ((far_own, 2 * width), BF16)],
        [1, 1, 1, 0, 0],
        [((rows, LANES), F32)],
        moved=4 * rows * width,
    )(base, center_shift, wide_shift, keys, values)

    came = swap(near, 1)
    step = 1
    while step < devices:
        far = jnp.concatenate([far, swap(far, step)], axis=0)
        step *= 2

    live = jnp.clip(valid_count - device * rows, 0, rows).astype(jnp.int32)
    product = 2 * rows * width
    p, qt, gt, kt, o1, top, total = call(
        functools.partial(forward_kernel, heads),
        [
            ((heads, rows, rows), BF16),
            ((width, rows), BF16),
            ((width, rows), BF16),
            ((width, rows), BF16),
            ((width, rows), F32),
            ((heads, rows), F32),
            ((heads, rows), F32),
        ],
        [1, 0, 0, 0, 0],
        [((width, rows), BF16)],
        flops=2 * product * rows * 5,
        moved=heads * rows * rows * 2,
    )(live, queries, keys, values, grad_out)

    own_at = device * rows
    near_at = jnp.arange(near_rows) * CENTER_DILATION
    slots = (jnp.arange(devices) ^ device)[:, None] * rows
    far_at = (slots + jnp.arange(far_own)[None, :] * WIDE_DILATION).reshape(-1)
    place = jnp.concatenate([own_at + near_at, (device ^ 1) * rows + near_at, far_at])
    place = jnp.broadcast_to(place.astype(jnp.int32)[:, None], (count, LANES))
    out, factor, delta, dq2, own, send, far_terms = call(
        functools.partial(remote_kernel, heads),
        [
            ((rows, width), BF16),
            ((heads, rows), F32),
            ((heads, rows), F32),
            ((width, rows), F32),
            ((near_rows, 2 * width), F32),
            ((near_rows, 2 * width), F32),
            ((far_rows, 2 * width), F32),
        ],
        [1, 1, 1, 1] + [0] * 9,
        [
            ((count, width), BF16),
            ((count, width), BF16),
            ((width, count), BF16),
            ((width, count), BF16),
            ((width, rows), F32),
            ((count, width), F32),
            ((count, width), F32),
        ],
        flops=6 * product * count * 5,
        moved=8 * rows * width,
    )(base, center_shift, wide_shift, valid_count, place, near, came, far, qt, gt, o1, top, total)

    back = swap(send, 1)
    step = devices // 2
    while step:
        half = far_own * step
        far_terms = far_terms[:half] + swap(far_terms[half:], step)
        step //= 2

    dq, dk, dv = call(
        functools.partial(backward_kernel, heads),
        [((rows, width), BF16), ((rows, width), F32), ((rows, width), F32)],
        [0] * 9,
        [((width, rows), F32)],
        flops=4 * product * rows * 5,
        moved=heads * rows * rows * 2,
    )(p, qt, gt, kt, keys, values, factor, delta, dq2)

    key_gradient, value_gradient = call(
        functools.partial(combine_kernel, heads),
        [((rows, width), BF16), ((rows, width), BF16)],
        [1, 1, 1, 0, 0, 0, 0, 0],
        [((rows, LANES), F32)],
        moved=12 * rows * width,
    )(base, center_shift, wide_shift, dk, dv, own, back, far_terms)
    return out, dq, key_gradient, value_gradient


def solution(mesh):
    split = P(("grp", "seq", "sub"), "hd")
    return jax.shard_map(
        local,
        mesh=mesh,
        in_specs=(split, split, split, split, P(), P(), P("grp")),
        out_specs=(split, split, split, split),
        check_vma=False,
    )
```

```python
import functools
import math

import jax
import jax.numpy as jnp
from jax import lax
from jax.experimental import pallas as pl
from jax.experimental.pallas import tpu as pltpu
from jax.sharding import PartitionSpec as P

HEAD_WIDTH = 48
CENTER_DILATION = 8
WIDE_DILATION = 128
LANES = 128
DEAD = -1e30
SCALE = HEAD_WIDTH**-0.5
EXP2_SCALE = SCALE * math.log2(math.e)
F32 = jnp.float32
BF16 = jnp.bfloat16

VMEM = pl.BlockSpec(memory_space=pltpu.VMEM)
SMEM = pl.BlockSpec(memory_space=pltpu.SMEM)


def nn(a, b):
    return jnp.dot(a, b, preferred_element_type=F32)


def nt(a, b):
    return lax.dot_general(a, b, (((1,), (1,)), ((), ())), preferred_element_type=F32)


def head_rows(h):
    return slice(h * HEAD_WIDTH, (h + 1) * HEAD_WIDTH)


def window(h):
    low = h * HEAD_WIDTH // LANES * LANES
    high = -(-(h + 1) * HEAD_WIDTH // LANES) * LANES
    return low, high


def embed(rows, h):
    low, high = window(h)
    before, after = h * HEAD_WIDTH - low, high - (h + 1) * HEAD_WIDTH
    parts = [rows]
    if before:
        parts.insert(0, jnp.zeros((before, rows.shape[1]), rows.dtype))
    if after:
        parts.append(jnp.zeros((after, rows.shape[1]), rows.dtype))
    return jnp.concatenate(parts, axis=0) if len(parts) > 1 else rows


def add_window(ref, h, value, started, at0):
    low, high = window(h)
    for at in range(low, high, LANES):
        part = value[:, at - low : at - low + LANES]
        here = slice(at - at0, at - at0 + LANES)
        if at in started:
            ref[:, here] += part
        else:
            started.add(at)
            ref[:, here] = part


def head_groups(heads):
    size = -(-heads // 3)
    groups = []
    for first in range(0, heads, size):
        last = min(first + size, heads)
        groups.append((first, last, window(first)[0], window(last - 1)[1]))
    return groups


def lane_shifts(shift_ref, base, heads, width):
    lane = lax.broadcasted_iota(jnp.int32, (1, width), 1)
    row = jnp.zeros((1, width), jnp.int32)
    for h in range(heads):
        inside = (lane >= h * HEAD_WIDTH) & (lane < (h + 1) * HEAD_WIDTH)
        row = jnp.where(inside, shift_ref[base + h], row)
    return row


def head_base(heads):
    return lax.axis_index("hd") * heads


def select_kernel(
    heads, valid_ref, center_any, wide_any, q_any, k_any, v_any, g_any,
    near_ref, far_ref, q_ref, k_ref, v_ref, g_ref, table_ref, lanes_ref,
    center_ref, wide_ref, spread_ref, sems,
):
    rows, width = k_ref.shape
    pairs = (
        (center_any, center_ref), (wide_any, wide_ref),
        (k_any, k_ref), (v_any, v_ref), (q_any, q_ref), (g_any, g_ref),
    )
    copies = [pltpu.make_async_copy(a, b, sems.at[i]) for i, (a, b) in enumerate(pairs)]
    for copy in copies:
        copy.start()
    for copy in copies[:2]:
        copy.wait()
    base = head_base(heads)
    center = lane_shifts(center_ref, base, heads, width)
    wide = lane_shifts(wide_ref, base, heads, width)
    lanes_ref[0:1, :] = center
    lanes_ref[1:2, :] = wide
    for h in range(heads):
        table_ref[h : h + 1, :] = jnp.full((1, rows), center_ref[base + h], jnp.int32)
        table_ref[heads + h : heads + h + 1, :] = jnp.full((1, rows), wide_ref[base + h], jnp.int32)
    table_ref[2 * heads : 2 * heads + 1, :] = jnp.full((1, rows), valid_ref[0], jnp.int32)
    near_rows = rows // CENTER_DILATION
    far_rows = rows // WIDE_DILATION
    row = lax.broadcasted_iota(jnp.int32, (far_rows, WIDE_DILATION, LANES), 1)
    for at, ref, copy in ((0, k_ref, copies[2]), (width, v_ref, copies[3])):
        copy.wait()
        for low in range(0, width, LANES):
            lanes = slice(low, low + LANES)
            packed = slice(at + low, at + low + LANES)
            spread = ref[:, lanes].astype(F32)
            spread_ref[at // width * (width // LANES) + low // LANES] = spread
            chosen = jnp.where(row == wide[:, lanes], spread.reshape(row.shape), 0.0)
            far_ref[:, packed] = jnp.sum(chosen, axis=1).astype(BF16)
    for at in (0, width):
        for low in range(0, width, LANES):
            lanes = slice(low, low + LANES)
            packed = slice(at + low, at + low + LANES)
            block = at // width * (width // LANES) + low // LANES
            picked = jnp.zeros((near_rows, LANES), F32)
            for step in range(CENTER_DILATION):
                rows_at = spread_ref[block, pl.ds(step, near_rows, stride=CENTER_DILATION), :]
                picked = jnp.where(center[:, lanes] == step, rows_at, picked)
            near_ref[:, packed] = picked.astype(BF16)
    copies[4].wait()
    copies[5].wait()


def forward_kernel(
    group, heads, q_ref, k_ref, v_ref, g_ref, table_ref, after_ref,
    p_ref, qt_ref, gt_ref, kt_ref, ot_ref, max_ref, sum_ref, vt_ref,
):
    first, last, low0, high0 = group
    rows = q_ref.shape[0]
    mine = slice(first * HEAD_WIDTH - low0, last * HEAD_WIDTH - low0)
    lanes0 = slice(low0, high0)
    qt_ref[...] = q_ref[:, lanes0].T[mine, :]
    vt_ref[...] = v_ref[:, lanes0].T[mine, :]
    device = lax.axis_index(("seq", "sub"))
    row = lax.broadcasted_iota(jnp.int32, (rows, LANES), 0)
    dead = jnp.where(device * rows + row < table_ref[2 * heads : 2 * heads + 1, :LANES], 0.0, DEAD)
    dead = jnp.concatenate([dead] * (rows // LANES), axis=1)

    def scores_of(h):
        low, high = window(h)
        return nn(k_ref[:, low:high], embed(qt_ref[head_rows(h - first), :], h))

    following = scores_of(first)
    for h in range(first, last):
        scores = following + dead
        if h + 1 < last:
            following = scores_of(h + 1)
        at = h - first
        is_near = (row & (CENTER_DILATION - 1)) == table_ref[h : h + 1, :LANES]
        is_far = (row & (WIDE_DILATION - 1)) == table_ref[heads + h : heads + h + 1, :LANES]
        times = 1.0 + is_near.astype(F32) + is_far.astype(F32)
        times = jnp.concatenate([times] * (rows // LANES), axis=1)
        top = jnp.max(scores, axis=0, keepdims=True)
        lifted = jnp.exp2((scores - top) * EXP2_SCALE) * times
        max_ref[at : at + 1, :] = top
        sum_ref[at : at + 1, :] = jnp.sum(lifted, axis=0, keepdims=True)
        weights = lifted.astype(BF16)
        p_ref[at] = weights
        ot_ref[head_rows(at), :] = nn(vt_ref[head_rows(at), :], weights)
    gt_ref[...] = g_ref[:, lanes0].T[mine, :]
    kt_ref[...] = k_ref[:, lanes0].T[mine, :]


def remote_kernel(heads, groups, far_own, table_ref, mine_ref, came_ref, *refs):
    parts = len(groups)
    qt_refs, gt_refs, o1_refs, max_refs, sum_refs = (refs[i * parts : (i + 1) * parts] for i in range(5))
    (
        ot_ref, factor_ref, delta_ref, ds_ref, kr_ref, keep_ref, send_ref,
        vr_ref, vrt_ref, dk_ref, dv_ref,
    ) = refs[5 * parts :]
    width, rows = ot_ref.shape
    half = came_ref.shape[0]
    near_rows = rows // CENTER_DILATION
    count = half + half - near_rows
    for at, ref in ((width, vr_ref), (0, kr_ref)):
        ref[:half, :] = came_ref[:, at : at + width]
        ref[half:, :] = mine_ref[near_rows:, at : at + width]
    vrt_ref[...] = vr_ref[...].T
    device = lax.axis_index(("seq", "sub"))
    row = lax.broadcasted_iota(jnp.int32, (count, LANES), 0)
    is_near = row < near_rows
    is_own = (row >= half) & (row < half + far_own)
    far_row = jnp.where(row < half, row - near_rows, row - half)
    slot = lax.shift_right_arithmetic(far_row, far_own.bit_length() - 1)
    code = 2 * slot + jnp.where(row < half, 1, 0)
    far_place = (device ^ code) * rows + (far_row & (far_own - 1)) * WIDE_DILATION
    place = jnp.where(is_near, (device ^ 1) * rows + row * CENTER_DILATION, far_place)
    room = jnp.where(is_own, -1, table_ref[2 * heads : 2 * heads + 1, :LANES] - place)
    began_k, began_v = set(), set()
    where = {}
    for part, (first, last, _, _) in enumerate(groups):
        for h in range(first, last):
            where[h] = part, h - first

    def products(h):
        low, high = window(h)
        part, at = where[h]
        q_rows = embed(qt_refs[part][head_rows(at), :], h)
        g_rows = embed(gt_refs[part][head_rows(at), :], h)
        return q_rows, g_rows, nn(kr_ref[:, low:high], q_rows), nn(vr_ref[:, low:high], g_rows)

    def forward(h, scores):
        part, at = where[h]
        shift = jnp.where(
            is_near, table_ref[h : h + 1, :LANES], table_ref[heads + h : heads + h + 1, :LANES]
        )
        dead = jnp.where(shift < room, 0.0, DEAD)
        scores = scores + jnp.concatenate([dead] * (rows // LANES), axis=1)
        top_here = max_refs[part][at : at + 1, :]
        top = jnp.maximum(jnp.max(scores, axis=0, keepdims=True), top_here)
        lifted = jnp.exp2((scores - top) * EXP2_SCALE)
        keep = jnp.exp2((top_here - top) * EXP2_SCALE)
        total = sum_refs[part][at : at + 1, :] * keep + jnp.sum(lifted, axis=0, keepdims=True)
        inverse = 1.0 / total
        prob = lifted * inverse
        factor = keep * inverse
        weights = prob.astype(BF16)
        return prob, weights, factor, nn(vrt_ref[head_rows(h), :], weights)

    def backward(h, q_rows, g_rows, grad_prob, prob, weights, factor, product):
        part, at = where[h]
        context = o1_refs[part][head_rows(at), :] * factor + product
        ot_ref[head_rows(h), :] = context.astype(BF16)
        g_head = gt_refs[part][head_rows(at), :].astype(F32)
        delta = jnp.sum(g_head * context, axis=0, keepdims=True)
        factor_ref[h : h + 1, :] = factor
        delta_ref[h : h + 1, :] = delta
        dscore = (prob * (grad_prob - delta)).astype(BF16)
        ds_ref[h] = dscore
        add_window(dk_ref, h, nt(dscore, q_rows), began_k, 0)
        add_window(dv_ref, h, nt(weights, g_rows), began_v, 0)

    made, done = {}, {}
    for step in range(heads + 2):
        if step < heads:
            made[step] = products(step)
        if 0 <= step - 1 < heads:
            done[step - 1] = forward(step - 1, made[step - 1][2])
        if 0 <= step - 2 < heads:
            q_rows, g_rows, _, grad_prob = made.pop(step - 2)
            backward(step - 2, q_rows, g_rows, grad_prob, *done.pop(step - 2))
    for at, ref, by in ((0, dk_ref, SCALE), (width, dv_ref, 1.0)):
        send_ref[:, at : at + width] = (ref[:half, :] * by).astype(send_ref.dtype)
        keep_ref[:, at : at + width] = ref[half:, :] * by


def backward_heads(
    group, p_ref, qt_ref, gt_ref, kt_ref, v_ref, kr_ref, ds2_ref, factor_ref, delta_ref,
    dqt_ref, dk_ref, dv_ref, krt_ref,
):
    first, last, low0, high0 = group
    mine = slice(first * HEAD_WIDTH - low0, last * HEAD_WIDTH - low0)
    krt_ref[...] = kr_ref[:, low0:high0].T[mine, :]
    began_k, began_v = set(), set()

    def products(h):
        low, high = window(h)
        g_rows = embed(gt_ref[head_rows(h - first), :], h)
        return g_rows, nn(v_ref[:, low:high], g_rows)

    following = products(first)
    for h in range(first, last):
        g_rows, grad_prob = following
        if h + 1 < last:
            following = products(h + 1)
        at = h - first
        q_rows = embed(qt_ref[head_rows(at), :], h)
        prob = p_ref[at].astype(F32) * factor_ref[h : h + 1, :]
        dscore = (prob * (grad_prob - delta_ref[h : h + 1, :])).astype(BF16)
        dqt = nn(krt_ref[head_rows(at), :], ds2_ref[h]) + nn(kt_ref[head_rows(at), :], dscore)
        dqt_ref[head_rows(at), :] = (dqt * SCALE).astype(BF16)
        add_window(dv_ref, h, nt(prob.astype(BF16), g_rows), began_v, low0)
        add_window(dk_ref, h, nt(dscore, q_rows), began_k, low0)


def first_backward_kernel(group, *refs):
    ot_ref, after_ref = refs[9:11]
    out_ref = refs[11]
    backward_heads(group, *refs[:9], *refs[12:])
    out_ref[...] = ot_ref[...].T


def middle_backward_kernel(group, *refs):
    backward_heads(group, *refs[:9], *refs[10:])


def last_backward_kernel(groups, *refs):
    others = len(groups) - 1
    lanes_ref, back_ref, after_ref = refs[9:12]
    terms = refs[12 : 12 + 3 * others]
    dq_ref, sum_ref, dqt_ref, dk_ref, dv_ref, krt_ref, turned_ref = refs[12 + 3 * others :]
    backward_heads(groups[-1], *refs[:9], dqt_ref, dk_ref, dv_ref, krt_ref)
    dqt_refs = (*terms[:others], dqt_ref)
    dk_refs = (*terms[others : 2 * others], dk_ref)
    dv_refs = (*terms[2 * others :], dv_ref)
    rows, width = dq_ref.shape
    near_rows = rows // CENTER_DILATION
    for (first, last, _, _), ref in zip(groups, dqt_refs):
        turned_ref[first * HEAD_WIDTH : last * HEAD_WIDTH, :] = ref[...]
    dq_ref[...] = turned_ref[...].T
    for at, parts, by in ((0, dk_refs, SCALE), (width, dv_refs, 1.0)):
        for low in range(0, width, LANES):
            block = (at + low) // LANES
            value = None
            for (_, _, low0, high0), ref in zip(groups, parts):
                if low0 <= low < high0:
                    term = ref[:, low - low0 : low - low0 + LANES]
                    value = term if value is None else value + term
            sum_ref[block] = value * by
            near = back_ref[:near_rows, at + low : at + low + LANES].astype(F32)
            center = lanes_ref[0:1, low : low + LANES]
            for step in range(CENTER_DILATION):
                strided = pl.ds(step, near_rows, stride=CENTER_DILATION)
                sum_ref[block, strided, :] += jnp.where(center == step, near, 0.0)


def combine_kernel(lanes_ref, sum_ref, far_ref, outk_ref, outv_ref):
    rows, width = outk_ref.shape
    far_rows = far_ref.shape[0]
    row = lax.broadcasted_iota(jnp.int32, (WIDE_DILATION, LANES), 0)
    for at, out in ((0, outk_ref), (width, outv_ref)):
        for low in range(0, width, LANES):
            block = (at + low) // LANES
            mask = row == lanes_ref[1:2, low : low + LANES]
            for index in range(far_rows):
                part = slice(index * WIDE_DILATION, (index + 1) * WIDE_DILATION)
                far = far_ref[index : index + 1, at + low : at + low + LANES]
                value = sum_ref[block, part, :] + jnp.where(mask, far, 0.0)
                out[part, low : low + LANES] = value.astype(BF16)


ANY = pl.BlockSpec(memory_space=pl.ANY)
HBM = pl.BlockSpec(memory_space=pltpu.HBM)


def call(body, outs, ins, scratch=(), flops=0, moved=0):
    return pl.pallas_call(
        body,
        out_shape=[jax.ShapeDtypeStruct(s, d) for s, d in outs],
        in_specs=ins,
        out_specs=[VMEM] * len(outs),
        scratch_shapes=list(scratch),
        compiler_params=pltpu.CompilerParams(vmem_limit_bytes=24 * 2**20),
        cost_estimate=pl.CostEstimate(flops=flops, bytes_accessed=moved, transcendentals=0),
    )


def local(queries, keys, values, grad_out, center_shift, wide_shift, valid_count):
    rows, width = queries.shape
    heads = width // HEAD_WIDTH
    groups = head_groups(heads)
    near_rows, far_own = rows // CENTER_DILATION, rows // WIDE_DILATION
    axes = ("seq", "sub")
    devices = lax.axis_size(axes)
    half = near_rows + far_own * devices // 2
    count = half + half - near_rows
    blocks = 2 * width // LANES
    order = [2**bit for bit in range(1, devices.bit_length() - 1)]

    def swap(value, apart):
        return lax.ppermute(value, axes, [(at, at ^ apart) for at in range(devices)])

    near, far, q, k, v, g, table, lanes = call(
        functools.partial(select_kernel, heads),
        [((near_rows, 2 * width), BF16), ((far_own, 2 * width), BF16)]
        + [((rows, width), BF16)] * 4
        + [((2 * heads + 8, rows), jnp.int32), ((8, width), jnp.int32)],
        [SMEM] + [HBM] * 6,
        [
            pltpu.SMEM(center_shift.shape, jnp.int32),
            pltpu.SMEM(wide_shift.shape, jnp.int32),
            pltpu.VMEM((blocks, rows, LANES), F32),
            pltpu.SemaphoreType.DMA((6,)),
        ],
        moved=16 * rows * width,
    )(
        valid_count,
        *(
            pltpu.with_memory_space_constraint(value, pltpu.HBM)
            for value in (center_shift, wide_shift, queries, keys, values, grad_out)
        )
    )

    def forward(index, after):
        first, last, _, _ = groups[index]
        size, tall = last - first, (last - first) * HEAD_WIDTH
        return call(
            functools.partial(forward_kernel, groups[index], heads),
            [
                ((size, rows, rows), BF16),
                ((tall, rows), BF16),
                ((tall, rows), BF16),
                ((tall, rows), BF16),
                ((tall, rows), F32),
                ((size, rows), F32),
                ((size, rows), F32),
            ],
            [VMEM] * 5 + [ANY],
            [pltpu.VMEM((tall, rows), BF16)],
            flops=2 * 2 * rows * rows * tall * 5,
            moved=size * rows * rows * 2,
        )(q, k, v, g, table, after)

    def in_step(run, sequence, after, transfers):
        results, left = {}, list(sequence)
        for start, finish in transfers:
            arrived = start()
            if left:
                index = left.pop(0)
                made = list(run(index, after, results))
                arrived, made[-1] = lax.optimization_barrier((arrived, made[-1]))
                results[index] = made
            finish(arrived)
            after = arrived
        for index in left:
            results[index] = run(index, after, results)
        return [results[index] for index in sorted(results)]

    box = {"far": far}

    def gather(step):
        def start():
            return swap(box["far"], step)

        def finish(arrived):
            box["far"] = jnp.concatenate([box["far"], arrived], axis=0)

        return start, finish

    def meet():
        box["mine"] = jnp.concatenate([near, box["far"]], axis=0)
        return swap(box["mine"], 1)

    def met(arrived):
        box["came"] = arrived

    parts = in_step(
        lambda index, after, _: forward(index, after),
        [len(groups) - 1, *range(len(groups) - 1)],
        far,
        [gather(step) for step in order] + [(meet, met)],
    )
    p, qt, gt, kt, o1, top, total = zip(*parts)

    ot, factor, delta, ds2, kr, keep, send = call(
        functools.partial(remote_kernel, heads, groups, far_own),
        [
            ((width, rows), BF16),
            ((heads, rows), F32),
            ((heads, rows), F32),
            ((heads, count, rows), BF16),
            ((count, width), BF16),
            ((count - half, 2 * width), F32),
            ((half, 2 * width), BF16),
        ],
        [VMEM] * (3 + 5 * len(groups)),
        [
            pltpu.VMEM((count, width), BF16),
            pltpu.VMEM((width, count), BF16),
            pltpu.VMEM((count, width), F32),
            pltpu.VMEM((count, width), F32),
        ],
        flops=5 * 2 * rows * width * count * 5,
        moved=8 * rows * width,
    )(table, box["mine"], box["came"], *qt, *gt, *o1, *top, *total)

    def meet_back():
        return swap(send, 1)

    def met_back(arrived):
        box["back"] = arrived
        box["terms"] = keep + arrived[near_rows:].astype(F32)

    def reduce(step):
        def start():
            return swap(box["terms"][box["terms"].shape[0] // 2 :], step)

        def finish(arrived):
            box["terms"] = box["terms"][: arrived.shape[0]] + arrived

        return start, finish

    def backward(index, after, results):
        first, last, low0, high0 = groups[index]
        size, tall = last - first, (last - first) * HEAD_WIDTH
        heads_in = (p[index], qt[index], gt[index], kt[index], v, kr, ds2, factor, delta)
        partial = [((tall, rows), BF16), ((rows, high0 - low0), F32), ((rows, high0 - low0), F32)]
        turned = pltpu.VMEM((tall, count), BF16)
        cost = dict(flops=4 * 2 * rows * rows * tall * 5, moved=size * rows * rows * 2)
        if index == 0:
            out, *terms = call(
                functools.partial(first_backward_kernel, groups[index]),
                [((rows, width), BF16), *partial],
                [VMEM] * 10 + [ANY],
                [turned],
                **cost,
            )(*heads_in, ot, after)
            box["out"] = out
            return terms
        if index < len(groups) - 1:
            return call(
                functools.partial(middle_backward_kernel, groups[index]),
                partial,
                [VMEM] * 9 + [ANY],
                [turned],
                **cost,
            )(*heads_in, after)
        others = [terms for _, terms in sorted(results.items())]
        return call(
            functools.partial(last_backward_kernel, groups),
            [((rows, width), BF16), ((blocks, rows, LANES), F32)],
            [VMEM] * 11 + [ANY] + [VMEM] * (3 * len(others)),
            [pltpu.VMEM(shape, dtype) for shape, dtype in partial]
            + [turned, pltpu.VMEM((width, rows), BF16)],
            **cost,
        )(*heads_in, lanes, box["back"], after, *[t[i] for i in range(3) for t in others])

    parts = in_step(
        backward, range(len(groups)), send, [(meet_back, met_back)] + [reduce(step) for step in reversed(order)]
    )
    dq, sums = parts[-1]
    key_gradient, value_gradient = call(
        combine_kernel,
        [((rows, width), BF16)] * 2,
        [VMEM] * 3,
        moved=12 * rows * width,
    )(lanes, sums, box["terms"])
    return box["out"], dq, key_gradient, value_gradient


def solution(mesh):
    split = P(("grp", "seq", "sub"), "hd")
    return jax.shard_map(
        local,
        mesh=mesh,
        in_specs=(split, split, split, split, P(), P(), P("grp")),
        out_specs=(split, split, split, split),
        check_vma=False,
    )
```

```python
import functools
import math

import jax
import jax.numpy as jnp
from jax import lax
from jax.experimental import pallas as pl
from jax.experimental.pallas import tpu as pltpu
from jax.sharding import PartitionSpec as P

HEAD_WIDTH = 48
CENTER_DILATION = 8
WIDE_DILATION = 128
LANES = 128
STACK = 256
ONES = 16
DEAD = -1e30
SCALE = HEAD_WIDTH**-0.5
EXP2_SCALE = SCALE * math.log2(math.e)
F32 = jnp.float32
BF16 = jnp.bfloat16

VMEM = pl.BlockSpec(memory_space=pltpu.VMEM)
SMEM = pl.BlockSpec(memory_space=pltpu.SMEM)


def nn(a, b):
    return jnp.dot(a, b, preferred_element_type=F32)


def nt(a, b):
    return lax.dot_general(a, b, (((1,), (1,)), ((), ())), preferred_element_type=F32)


def head_rows(h):
    return slice(h * HEAD_WIDTH, (h + 1) * HEAD_WIDTH)


def window(h):
    low = h * HEAD_WIDTH // LANES * LANES
    high = -(-(h + 1) * HEAD_WIDTH // LANES) * LANES
    return low, high


def embed(rows, h):
    low, high = window(h)
    before, after = h * HEAD_WIDTH - low, high - (h + 1) * HEAD_WIDTH
    parts = [rows]
    if before:
        parts.insert(0, jnp.zeros((before, rows.shape[1]), rows.dtype))
    if after:
        parts.append(jnp.zeros((after, rows.shape[1]), rows.dtype))
    return jnp.concatenate(parts, axis=0) if len(parts) > 1 else rows


def head_groups(heads):
    size = -(-heads // 3)
    groups = []
    for first in range(0, heads, size):
        last = min(first + size, heads)
        groups.append((first, last, window(first)[0], window(last - 1)[1]))
    return groups


def lane_shifts(shift_ref, base, heads, width):
    lane = lax.broadcasted_iota(jnp.int32, (1, width), 1)
    row = jnp.zeros((1, width), jnp.int32)
    for h in range(heads):
        inside = (lane >= h * HEAD_WIDTH) & (lane < (h + 1) * HEAD_WIDTH)
        row = jnp.where(inside, shift_ref[base + h], row)
    return row


def head_base(heads):
    return lax.axis_index("hd") * heads


def select_kernel(
    heads, center_any, wide_any, q_any, k_any, v_any, g_any,
    near_ref, far_ref, q_ref, k_ref, v_ref, g_ref, table_ref, lanes_ref,
    center_ref, wide_ref, spread_ref, sems,
):
    rows, width = k_ref.shape
    pairs = (
        (center_any, center_ref), (wide_any, wide_ref),
        (k_any, k_ref), (v_any, v_ref), (q_any, q_ref), (g_any, g_ref),
    )
    copies = [pltpu.make_async_copy(a, b, sems.at[i]) for i, (a, b) in enumerate(pairs)]
    for copy in copies:
        copy.start()
    for copy in copies[:2]:
        copy.wait()
    base = head_base(heads)
    center = lane_shifts(center_ref, base, heads, width)
    wide = lane_shifts(wide_ref, base, heads, width)
    lanes_ref[0:1, :] = center
    lanes_ref[1:2, :] = wide
    for h in range(heads):
        table_ref[h : h + 1, :] = jnp.full((1, rows), center_ref[base + h], jnp.int32)
        table_ref[heads + h : heads + h + 1, :] = jnp.full((1, rows), wide_ref[base + h], jnp.int32)
    near_rows = rows // CENTER_DILATION
    far_rows = rows // WIDE_DILATION
    row = lax.broadcasted_iota(jnp.int32, (far_rows, WIDE_DILATION, LANES), 1)
    for at, ref, copy in ((0, k_ref, copies[2]), (width, v_ref, copies[3])):
        copy.wait()
        for low in range(0, width, LANES):
            lanes = slice(low, low + LANES)
            packed = slice(at + low, at + low + LANES)
            spread = ref[:, lanes].astype(F32)
            spread_ref[at // width * (width // LANES) + low // LANES] = spread
            chosen = jnp.where(row == wide[:, lanes], spread.reshape(row.shape), 0.0)
            far_ref[:, packed] = jnp.sum(chosen, axis=1).astype(BF16)
    for at in (0, width):
        for low in range(0, width, LANES):
            lanes = slice(low, low + LANES)
            packed = slice(at + low, at + low + LANES)
            block = at // width * (width // LANES) + low // LANES
            picked = jnp.zeros((near_rows, LANES), F32)
            for step in range(CENTER_DILATION):
                rows_at = spread_ref[block, pl.ds(step, near_rows, stride=CENTER_DILATION), :]
                picked = jnp.where(center[:, lanes] == step, rows_at, picked)
            near_ref[:, packed] = picked.astype(BF16)
    copies[4].wait()
    copies[5].wait()


def forward_heads(
    group, heads, valid_ref, table_ref, k_ref, qt_ref, vt_ref, p_ref, ot_ref, max_ref, sum_ref
):
    first, last, _, _ = group
    rows = k_ref.shape[0]
    device = lax.axis_index(("seq", "sub"))
    row = lax.broadcasted_iota(jnp.int32, (rows, LANES), 0)
    dead = jnp.where(device * rows + row < valid_ref[0], 0.0, DEAD)
    ones = jnp.ones((ONES, rows), BF16)

    def scores_of(h):
        low, high = window(h)
        is_near = (row & (CENTER_DILATION - 1)) == table_ref[h : h + 1, :LANES]
        is_far = (row & (WIDE_DILATION - 1)) == table_ref[heads + h : heads + h + 1, :LANES]
        once = jnp.where(is_near | is_far, 1.0 / EXP2_SCALE, 0.0)
        bias = dead + jnp.where(is_near & is_far, math.log2(3) / EXP2_SCALE, once)
        scores = nn(k_ref[:, low:high], embed(qt_ref[head_rows(h), :], h)) + widen(bias, rows)
        return scores, jnp.max(scores, axis=0, keepdims=True)

    following = scores_of(first)
    for h in range(first, last):
        scores, top = following
        if h + 1 < last:
            following = scores_of(h + 1)
        at = h - first
        weights = jnp.exp2((scores - top) * EXP2_SCALE).astype(BF16)
        p_ref[at] = weights
        summed = nn(jnp.concatenate([vt_ref[head_rows(h), :], ones], axis=0), weights)
        max_ref[at : at + 1, :] = top
        sum_ref[at : at + 1, :] = summed[HEAD_WIDTH : HEAD_WIDTH + 1]
        ot_ref[head_rows(at), :] = summed[:HEAD_WIDTH]


def first_forward_kernel(
    group, heads, valid_ref, table_ref, k_ref, q_ref, v_ref, g_ref, after_ref,
    qt_ref, gt_ref, kt_ref, vt_ref, *outs,
):
    qt_ref[...] = q_ref[...].T
    vt_ref[...] = v_ref[...].T
    forward_heads(group, heads, valid_ref, table_ref, k_ref, qt_ref, vt_ref, *outs)
    gt_ref[...] = g_ref[...].T
    kt_ref[...] = k_ref[...].T


def forward_kernel(group, heads, valid_ref, table_ref, k_ref, qt_ref, vt_ref, after_ref, *outs):
    forward_heads(group, heads, valid_ref, table_ref, k_ref, qt_ref, vt_ref, *outs)


def stacks(heads, count):
    size = max(1, min(heads, STACK // count))
    found = []
    for first in range(0, heads, size):
        last = min(first + size, heads)
        found.append((first, last, window(first)[0], window(last - 1)[1]))
    return found


def head_lanes(h, low, high):
    lane = low + lax.broadcasted_iota(jnp.int32, (1, high - low), 1)
    return (lane >= h * HEAD_WIDTH) & (lane < (h + 1) * HEAD_WIDTH)


def stacked(rows, stack):
    first, last, low, high = stack
    return jnp.concatenate(
        [rows[:, low:high] * head_lanes(h, low, high).astype(F32).astype(BF16) for h in range(first, last)],
        axis=0,
    )


def unstack(ref, at0, stack, count, value, by, started):
    first, last, low, high = stack
    total = None
    for at, h in enumerate(range(first, last)):
        part = jnp.where(head_lanes(h, low, high), value[at * count : (at + 1) * count], 0.0)
        total = part if total is None else total + part
    total = total * by
    for at in range(low, high, LANES):
        part = total[:, at - low : at - low + LANES]
        if (at0, at) in started:
            ref[:, at0 + at : at0 + at + LANES] += part
        else:
            started.add((at0, at))
            ref[:, at0 + at : at0 + at + LANES] = part


def widen(value, rows):
    return jnp.concatenate([value] * (rows // LANES), axis=1)


def near_forward_kernel(heads, groups, valid_ref, table_ref, near_ref, qt_ref, *refs):
    parts = len(groups)
    o1_refs, max_refs, sum_refs = (refs[i * parts : (i + 1) * parts] for i in range(3))
    after_ref, p_ref, o_ref, old_ref, top_ref, sum_ref = refs[3 * parts :]
    width, rows = qt_ref.shape
    count = near_ref.shape[0]
    device = lax.axis_index(("seq", "sub"))
    row = lax.broadcasted_iota(jnp.int32, (count, LANES), 0)
    room = valid_ref[0] - ((device ^ 1) * rows + row * CENTER_DILATION)
    where = {}
    for part, (first, last, _, _) in enumerate(groups):
        for h in range(first, last):
            where[h] = part, h - first
    for stack in stacks(heads, count):
        first, last, low, high = stack
        scores = nn(stacked(near_ref[:, :width], stack), qt_ref[low:high, :])
        lifts, keeps = [], []
        for at, h in enumerate(range(first, last)):
            part, index = where[h]
            dead = jnp.where(table_ref[h : h + 1, :LANES] < room, 0.0, DEAD)
            here = scores[at * count : (at + 1) * count] + widen(dead, rows)
            old = max_refs[part][index : index + 1, :]
            top = jnp.maximum(jnp.max(here, axis=0, keepdims=True), old)
            lifted = jnp.exp2((here - top) * EXP2_SCALE)
            keep = jnp.exp2((old - top) * EXP2_SCALE)
            old_ref[h : h + 1, :] = old
            top_ref[h : h + 1, :] = top
            sum_ref[h : h + 1, :] = sum_refs[part][index : index + 1, :] * keep + jnp.sum(
                lifted, axis=0, keepdims=True
            )
            keeps.append(keep)
            lifts.append(lifted.astype(BF16))
        weights = jnp.concatenate(lifts, axis=0)
        p_ref[first * count : last * count, :] = weights
        added = nn(stacked(near_ref[:, width:], stack).T, weights)
        for keep, h in zip(keeps, range(first, last)):
            part, index = where[h]
            inside = added[h * HEAD_WIDTH - low : (h + 1) * HEAD_WIDTH - low]
            o_ref[head_rows(h), :] = o1_refs[part][head_rows(index), :] * keep + inside


def wide_kernel(
    heads, far_own, valid_ref, table_ref, far_ref, qt_ref, gt_ref, o_ref, old_ref, near_top_ref, near_sum_ref,
    ot_ref, local_ref, near_ref, delta_ref, ds_ref, keep_ref, send_ref, sum_ref,
):
    width, rows = qt_ref.shape
    count = far_ref.shape[0]
    half = count // 2
    device = lax.axis_index(("seq", "sub"))
    row = lax.broadcasted_iota(jnp.int32, (count, LANES), 0)
    slot = lax.shift_right_arithmetic(row, far_own.bit_length() - 1)
    place = (device ^ slot) * rows + (row & (far_own - 1)) * WIDE_DILATION
    room = jnp.where(slot == 0, -1, valid_ref[0] - place)
    started = set()
    for stack in stacks(heads, count):
        first, last, low, high = stack
        value_rows = stacked(far_ref[:, width:], stack)
        scores = nn(stacked(far_ref[:, :width], stack), qt_ref[low:high, :])
        grad_prob = nn(value_rows, gt_ref[low:high, :])
        probs, factors = [], []
        for at, h in enumerate(range(first, last)):
            one = slice(h, h + 1)
            dead = jnp.where(table_ref[heads + h : heads + h + 1, :LANES] < room, 0.0, DEAD)
            here = scores[at * count : (at + 1) * count] + widen(dead, rows)
            near_top = near_top_ref[one, :]
            top = jnp.maximum(jnp.max(here, axis=0, keepdims=True), near_top)
            lifted = jnp.exp2((here - top) * EXP2_SCALE)
            keep = jnp.exp2((near_top - top) * EXP2_SCALE)
            inverse = 1.0 / (near_sum_ref[one, :] * keep + jnp.sum(lifted, axis=0, keepdims=True))
            probs.append(lifted * inverse)
            factors.append(keep * inverse)
            near_ref[one, :] = keep * inverse
            local_ref[one, :] = jnp.exp2((old_ref[one, :] - top) * EXP2_SCALE) * inverse
        weights = jnp.concatenate([prob.astype(BF16) for prob in probs], axis=0)
        added = nn(value_rows.T, weights)
        dscores = []
        for at, h in enumerate(range(first, last)):
            inside = added[h * HEAD_WIDTH - low : (h + 1) * HEAD_WIDTH - low]
            context = o_ref[head_rows(h), :] * factors[at] + inside
            ot_ref[head_rows(h), :] = context.astype(BF16)
            delta = jnp.sum(gt_ref[head_rows(h), :].astype(F32) * context, axis=0, keepdims=True)
            delta_ref[h : h + 1, :] = delta
            here = grad_prob[at * count : (at + 1) * count]
            dscores.append((probs[at] * (here - delta)).astype(BF16))
        dscore = jnp.concatenate(dscores, axis=0)
        ds_ref[first * count : last * count, :] = dscore
        unstack(sum_ref, 0, stack, count, nt(dscore, qt_ref[low:high, :]), SCALE, started)
        unstack(sum_ref, width, stack, count, nt(weights, gt_ref[low:high, :]), 1.0, started)
    keep_ref[...] = sum_ref[:half, :]
    send_ref[...] = sum_ref[half:, :].astype(send_ref.dtype)


def near_backward_kernel(
    heads, near_ref, far_ref, qt_ref, gt_ref, p_ref, ds_ref, factor_ref, delta_ref, ot_ref, after_ref,
    out_ref, dq_ref, send_ref, sum_ref,
):
    width, rows = qt_ref.shape
    count = near_ref.shape[0]
    started, begun = set(), set()

    def add_dq(stack, product):
        first, last, low, _ = stack
        for h in range(first, last):
            inside = product[h * HEAD_WIDTH - low : (h + 1) * HEAD_WIDTH - low]
            if h in begun:
                dq_ref[head_rows(h), :] += inside
            else:
                begun.add(h)
                dq_ref[head_rows(h), :] = inside

    for stack in stacks(heads, count):
        first, last, low, high = stack
        grad_prob = nn(stacked(near_ref[:, width:], stack), gt_ref[low:high, :])
        weights, dscores = [], []
        for at, h in enumerate(range(first, last)):
            prob = p_ref[h * count : (h + 1) * count, :].astype(F32) * factor_ref[h : h + 1, :]
            here = grad_prob[at * count : (at + 1) * count]
            weights.append(prob.astype(BF16))
            dscores.append((prob * (here - delta_ref[h : h + 1, :])).astype(BF16))
        dscore = jnp.concatenate(dscores, axis=0)
        add_dq(stack, nn(stacked(near_ref[:, :width], stack).T, dscore))
        unstack(sum_ref, 0, stack, count, nt(dscore, qt_ref[low:high, :]), SCALE, started)
        weight = jnp.concatenate(weights, axis=0)
        unstack(sum_ref, width, stack, count, nt(weight, gt_ref[low:high, :]), 1.0, started)
    send_ref[...] = sum_ref[...].astype(send_ref.dtype)
    count = far_ref.shape[0]
    for stack in stacks(heads, count):
        first, last, _, _ = stack
        dscore = ds_ref[first * count : last * count, :]
        add_dq(stack, nn(stacked(far_ref[:, :width], stack).T, dscore))
    out_ref[...] = ot_ref[...].T


def backward_heads(
    group, p_ref, qt_ref, gt_ref, kt_ref, v_ref, dq2_ref, factor_ref, delta_ref, dqt_ref, dk_ref, dv_ref
):
    first, last, _, _ = group
    rows = v_ref.shape[0]
    parts = [slice(at, at + rows // 2) for at in (0, rows // 2)]
    work = [(h, part) for h in range(first, last) for part in parts]

    def product(h, part):
        low, high = window(h)
        return nn(v_ref[part, low:high], embed(gt_ref[head_rows(h), :], h))

    following = product(*work[0])
    for index, (h, part) in enumerate(work):
        grad_prob = following
        if index + 1 < len(work):
            following = product(*work[index + 1])
        at, head = h - first, head_rows(h)
        here = head_rows(at)
        prob = p_ref[at, part, :].astype(F32) * factor_ref[h : h + 1, :]
        dv_ref[here, part] = nt(gt_ref[head, :], prob.astype(BF16))
        dscore = (prob * (grad_prob - delta_ref[h : h + 1, :])).astype(BF16)
        dk_ref[here, part] = nt(qt_ref[head, :], dscore)
        term = nn(kt_ref[head, part], dscore)
        dqt = term + (dq2_ref[head, :] if part is parts[0] else dqt)
        if part is parts[1]:
            dqt_ref[here, :] = (dqt * SCALE).astype(BF16)


def backward_kernel(group, *refs):
    backward_heads(group, *refs[:8], *refs[9:])


def last_backward_kernel(groups, index, *refs):
    others = len(groups) - 1
    lanes_ref, back_ref, after_ref = refs[8:11]
    terms = refs[11 : 11 + 3 * others]
    dq_ref, sum_ref, dqt_ref, dk_ref, dv_ref, turned_ref, wide_ref = refs[11 + 3 * others :]
    backward_heads(groups[index], *refs[:8], dqt_ref, dk_ref, dv_ref)

    def all_groups(at, mine):
        found = list(terms[at * others : (at + 1) * others])
        found.insert(index, mine)
        return found

    rows, width = dq_ref.shape
    near_rows = rows // CENTER_DILATION
    for (first, last, _, _), ref in zip(groups, all_groups(0, dqt_ref)):
        turned_ref[first * HEAD_WIDTH : last * HEAD_WIDTH, :] = ref[...]
    dq_ref[...] = turned_ref[...].T
    for at, parts, by in ((0, all_groups(1, dk_ref), SCALE), (width, all_groups(2, dv_ref), 1.0)):
        for (first, last, _, _), ref in zip(groups, parts):
            wide_ref[first * HEAD_WIDTH : last * HEAD_WIDTH, :] = ref[...] * by
        for low in range(0, width, LANES):
            block = (at + low) // LANES
            sum_ref[block] = wide_ref[low : low + LANES, :].T
            near = back_ref[:, at + low : at + low + LANES].astype(F32)
            center = lanes_ref[0:1, low : low + LANES]
            for step in range(CENTER_DILATION):
                strided = pl.ds(step, near_rows, stride=CENTER_DILATION)
                sum_ref[block, strided, :] += jnp.where(center == step, near, 0.0)


def combine_kernel(lanes_ref, sum_ref, far_ref, outk_ref, outv_ref):
    rows, width = outk_ref.shape
    far_rows = far_ref.shape[0]
    row = lax.broadcasted_iota(jnp.int32, (WIDE_DILATION, LANES), 0)
    for at, out in ((0, outk_ref), (width, outv_ref)):
        for low in range(0, width, LANES):
            block = (at + low) // LANES
            mask = row == lanes_ref[1:2, low : low + LANES]
            for index in range(far_rows):
                part = slice(index * WIDE_DILATION, (index + 1) * WIDE_DILATION)
                far = far_ref[index : index + 1, at + low : at + low + LANES]
                value = sum_ref[block, part, :] + jnp.where(mask, far, 0.0)
                out[part, low : low + LANES] = value.astype(BF16)


ANY = pl.BlockSpec(memory_space=pl.ANY)
HBM = pl.BlockSpec(memory_space=pltpu.HBM)


def call(body, outs, ins, scratch=(), *, flops=0, moved=0):
    return pl.pallas_call(
        body,
        out_shape=[jax.ShapeDtypeStruct(s, d) for s, d in outs],
        in_specs=ins,
        out_specs=[VMEM] * len(outs),
        scratch_shapes=list(scratch),
        compiler_params=pltpu.CompilerParams(vmem_limit_bytes=24 * 2**20),
        cost_estimate=pl.CostEstimate(flops=flops, bytes_accessed=moved, transcendentals=0),
    )


def local(queries, keys, values, grad_out, center_shift, wide_shift, valid_count):
    rows, width = queries.shape
    heads = width // HEAD_WIDTH
    groups = head_groups(heads)
    near_rows, far_own = rows // CENTER_DILATION, rows // WIDE_DILATION
    axes = ("seq", "sub")
    devices = lax.axis_size(axes)
    far_rows = far_own * devices
    blocks = 2 * width // LANES
    steps = [2**bit for bit in range(devices.bit_length() - 1)]

    def swap(value, apart):
        return lax.ppermute(value, axes, [(at, at ^ apart) for at in range(devices)])

    near, far, q, k, v, g, table, lanes = call(
        functools.partial(select_kernel, heads),
        [((near_rows, 2 * width), BF16), ((far_own, 2 * width), BF16)]
        + [((rows, width), BF16)] * 4
        + [((2 * heads, rows), jnp.int32), ((8, width), jnp.int32)],
        [HBM] * 6,
        [
            pltpu.SMEM(center_shift.shape, jnp.int32),
            pltpu.SMEM(wide_shift.shape, jnp.int32),
            pltpu.VMEM((blocks, rows, LANES), F32),
            pltpu.SemaphoreType.DMA((6,)),
        ],
        moved=16 * rows * width,
    )(
        *(
            pltpu.with_memory_space_constraint(value, pltpu.HBM)
            for value in (center_shift, wide_shift, queries, keys, values, grad_out)
        )
    )

    valid, far = lax.optimization_barrier((valid_count, far))

    def cost(heads_done, keys_done, products):
        done = heads_done * keys_done * rows
        return dict(flops=2 * HEAD_WIDTH * done * products * 5, moved=2 * done)

    turned = {}
    fronts = {}

    def front(index, after):
        first, last, _, _ = groups[index]
        size, tall = last - first, (last - first) * HEAD_WIDTH
        outs = [((size, rows, rows), BF16), ((tall, rows), F32), ((size, rows), F32), ((size, rows), F32)]
        if not turned:
            *flipped, p, o, top, total = call(
                functools.partial(first_forward_kernel, groups[index], heads),
                [((width, rows), BF16)] * 4 + outs,
                [SMEM] + [VMEM] * 5 + [ANY],
                **cost(size, rows, 2),
            )(valid, table, k, q, v, g, after)
            turned.update(zip(("qt", "gt", "kt", "vt"), flipped))
        else:
            p, o, top, total = call(
                functools.partial(forward_kernel, groups[index], heads),
                outs,
                [SMEM] + [VMEM] * 4 + [ANY],
                **cost(size, rows, 2),
            )(valid, table, k, turned["qt"], turned["vt"], after)
        fronts[index] = [p, o, top, total]

    def tie(arrived, holder, key):
        arrived, held = lax.optimization_barrier((arrived, holder[key][-1]))
        holder[key] = [*holder[key][:-1], held]
        return arrived

    last = len(groups) - 1
    order = [last, *range(last)]
    after = far
    for at, step in enumerate(steps):
        arrived = swap(far, step)
        if at == 0:
            near_came = swap(near, 1)
        if at < len(order):
            front(order[at], after)
        if at == len(order) - 1:
            p, o, top, total = zip(*(fronts[index] for index in range(len(groups))))
            fronts["near"] = call(
                functools.partial(near_forward_kernel, heads, groups),
                [((heads * near_rows, rows), BF16), ((width, rows), F32)] + [((heads, rows), F32)] * 3,
                [SMEM] + [VMEM] * (3 + 3 * len(groups)) + [ANY],
                **cost(heads, near_rows, 2),
            )(valid, table, near_came, turned["qt"], *o, *top, *total, after)
            arrived = tie(arrived, fronts, "near")
        elif at < len(order):
            arrived = tie(arrived, fronts, order[at])
        after = arrived
        far = jnp.concatenate([far, arrived], axis=0)
    near_p, o, old, near_top, near_sum = fronts["near"]
    qt, gt, kt = (turned[name] for name in ("qt", "gt", "kt"))

    ot, local_factor, near_factor, delta, ds, terms, send = call(
        functools.partial(wide_kernel, heads, far_own),
        [((width, rows), BF16)]
        + [((heads, rows), F32)] * 3
        + [((heads * far_rows, rows), BF16)]
        + [((far_rows // 2, 2 * width), F32)] * 2,
        [SMEM] + [VMEM] * 8,
        [pltpu.VMEM((far_rows, 2 * width), F32)],
        **cost(heads, far_rows, 5),
    )(valid, table, far, qt, gt, o, old, near_top, near_sum)

    backs = {}

    def back(index, after):
        first, end, _, _ = groups[index]
        size, tall = end - first, (end - first) * HEAD_WIDTH
        partial = [((tall, rows), BF16), ((tall, rows), F32), ((tall, rows), F32)]
        given = (p[index], qt, gt, kt, v, backs["near"][1], local_factor, delta)
        if len(backs) < len(groups):
            backs[index] = call(
                functools.partial(backward_kernel, groups[index]),
                partial,
                [VMEM] * 8 + [ANY],
                **cost(size, rows, 4),
            )(*given, after)
            return
        others = [backs[other] for other in range(len(groups)) if other != index]
        backs[index] = call(
            functools.partial(last_backward_kernel, groups, index),
            [((rows, width), BF16), ((blocks, rows, LANES), F32)],
            [VMEM] * 10 + [ANY] + [VMEM] * (3 * len(others)),
            [pltpu.VMEM(shape, dtype) for shape, dtype in partial]
            + [pltpu.VMEM((width, rows), BF16), pltpu.VMEM((width, rows), F32)],
            **cost(size, rows, 4),
        )(*given, lanes, near_back, after, *[terms[i] for i in range(3) for terms in others])

    after = send
    for at, step in enumerate(reversed(steps)):
        if at:
            half = terms.shape[0] // 2
            send, terms = terms[half:], terms[:half]
        arrived = swap(send, step)
        if at == 0:
            backs["near"] = call(
                functools.partial(near_backward_kernel, heads),
                [((rows, width), BF16), ((width, rows), F32), ((near_rows, 2 * width), BF16)],
                [VMEM] * 9 + [ANY],
                [pltpu.VMEM((near_rows, 2 * width), F32)],
                **cost(heads, near_rows, 4),
            )(near_came, far, qt, gt, near_p, ds, near_factor, delta, ot, after)
        if at == 1:
            near_back = swap(backs["near"][2], 1)
        if at < len(order):
            back(order[at], after)
            arrived = tie(arrived, backs, order[at])
        after = arrived
        terms = terms + arrived.astype(F32)

    dq, sums = backs[order[-1]]
    key_gradient, value_gradient = call(
        combine_kernel,
        [((rows, width), BF16)] * 2,
        [VMEM] * 3,
        moved=12 * rows * width,
    )(lanes, sums, terms)
    return backs["near"][0], dq, key_gradient, value_gradient


def solution(mesh):
    split = P(("grp", "seq", "sub"), "hd")
    return jax.shard_map(
        local,
        mesh=mesh,
        in_specs=(split, split, split, split, P(), P(), P("grp")),
        out_specs=(split, split, split, split),
        check_vma=False,
    )
```

```python
import functools
import math

import jax
import jax.numpy as jnp
from jax import lax
from jax.experimental import pallas as pl
from jax.experimental.pallas import tpu as pltpu
from jax.sharding import PartitionSpec as P

HEAD_WIDTH = 48
CENTER_DILATION = 8
WIDE_DILATION = 128
LANES = 128
STACK = 256
ONES = 16
OUT_AT = 2
DEAD = -1e30
SCALE = HEAD_WIDTH**-0.5
EXP2_SCALE = SCALE * math.log2(math.e)
F32 = jnp.float32
BF16 = jnp.bfloat16

VMEM = pl.BlockSpec(memory_space=pltpu.VMEM)
SMEM = pl.BlockSpec(memory_space=pltpu.SMEM)


def nn(a, b):
    return jnp.dot(a, b, preferred_element_type=F32)


def nt(a, b):
    return lax.dot_general(a, b, (((1,), (1,)), ((), ())), preferred_element_type=F32)


def head_rows(h):
    return slice(h * HEAD_WIDTH, (h + 1) * HEAD_WIDTH)


def window(h):
    low = h * HEAD_WIDTH // LANES * LANES
    high = -(-(h + 1) * HEAD_WIDTH // LANES) * LANES
    return low, high


def embed(rows, h):
    low, high = window(h)
    before, after = h * HEAD_WIDTH - low, high - (h + 1) * HEAD_WIDTH
    parts = [rows]
    if before:
        parts.insert(0, jnp.zeros((before, rows.shape[1]), rows.dtype))
    if after:
        parts.append(jnp.zeros((after, rows.shape[1]), rows.dtype))
    return jnp.concatenate(parts, axis=0) if len(parts) > 1 else rows


def head_groups(heads):
    edge = max(1, heads // 4)
    return [(0, edge), (edge, heads - edge), (heads - edge, heads)]


def lane_shifts(shift_ref, base, heads, width):
    lane = lax.broadcasted_iota(jnp.int32, (1, width), 1)
    row = jnp.zeros((1, width), jnp.int32)
    for h in range(heads):
        inside = (lane >= h * HEAD_WIDTH) & (lane < (h + 1) * HEAD_WIDTH)
        row = jnp.where(inside, shift_ref[base + h], row)
    return row


def head_base(heads):
    return lax.axis_index("hd") * heads


def select_kernel(
    heads, center_any, wide_any, q_any, k_any, v_any, g_any,
    far_ref, q_ref, k_ref, v_ref, g_ref, table_ref, lanes_ref,
    center_ref, wide_ref, sems,
):
    rows, width = k_ref.shape
    pairs = (
        (center_any, center_ref), (wide_any, wide_ref),
        (k_any, k_ref), (v_any, v_ref), (q_any, q_ref), (g_any, g_ref),
    )
    copies = [pltpu.make_async_copy(a, b, sems.at[i]) for i, (a, b) in enumerate(pairs)]
    for copy in copies:
        copy.start()
    for copy in copies[:2]:
        copy.wait()
    base = head_base(heads)
    center = lane_shifts(center_ref, base, heads, width)
    wide = lane_shifts(wide_ref, base, heads, width)
    lanes_ref[0:1, :] = center
    lanes_ref[1:2, :] = wide
    for h in range(heads):
        table_ref[h : h + 1, :] = jnp.full((1, rows), center_ref[base + h], jnp.int32)
        table_ref[heads + h : heads + h + 1, :] = jnp.full((1, rows), wide_ref[base + h], jnp.int32)
    far_rows = rows // WIDE_DILATION
    row = lax.broadcasted_iota(jnp.int32, (far_rows, WIDE_DILATION, LANES), 1)
    for at, ref, copy in ((0, k_ref, copies[2]), (width, v_ref, copies[3])):
        copy.wait()
        for low in range(0, width, LANES):
            lanes = slice(low, low + LANES)
            packed = slice(at + low, at + low + LANES)
            spread = ref[:, lanes].astype(F32)
            chosen = jnp.where(row == wide[:, lanes], spread.reshape(row.shape), 0.0)
            far_ref[:, packed] = jnp.sum(chosen, axis=1).astype(BF16)
    copies[4].wait()
    copies[5].wait()


def forward_heads(
    group, heads, valid_ref, table_ref, k_ref, qt_ref, vt_ref, p_ref, ot_ref, max_ref, sum_ref
):
    first, last = group
    rows = k_ref.shape[0]
    device = lax.axis_index(("seq", "sub"))
    row = lax.broadcasted_iota(jnp.int32, (rows, LANES), 0)
    dead = jnp.where(device * rows + row < valid_ref[0], 0.0, DEAD)
    ones = jnp.ones((ONES, rows), BF16)

    def scores_of(h):
        low, high = window(h)
        is_near = (row & (CENTER_DILATION - 1)) == table_ref[h : h + 1, :LANES]
        is_far = (row & (WIDE_DILATION - 1)) == table_ref[heads + h : heads + h + 1, :LANES]
        once = jnp.where(is_near | is_far, 1.0 / EXP2_SCALE, 0.0)
        bias = dead + jnp.where(is_near & is_far, math.log2(3) / EXP2_SCALE, once)
        scores = nn(k_ref[:, low:high], embed(qt_ref[head_rows(h), :], h)) + widen(bias, rows)
        return scores, jnp.max(scores, axis=0, keepdims=True)

    following = scores_of(first)
    for h in range(first, last):
        scores, top = following
        if h + 1 < last:
            following = scores_of(h + 1)
        at = h - first
        weights = jnp.exp2((scores - top) * EXP2_SCALE).astype(BF16)
        p_ref[at] = weights
        summed = nn(jnp.concatenate([vt_ref[head_rows(h), :], ones], axis=0), weights)
        max_ref[at : at + 1, :] = top
        sum_ref[at : at + 1, :] = summed[HEAD_WIDTH : HEAD_WIDTH + 1]
        ot_ref[head_rows(at), :] = summed[:HEAD_WIDTH]


def select_near(center_ref, source_ref, near_ref, at0, spread_ref):
    rows, width = source_ref.shape
    near_rows = rows // CENTER_DILATION
    for low in range(0, width, LANES):
        lanes = slice(low, low + LANES)
        spread_ref[low // LANES] = source_ref[:, lanes].astype(F32)
    for low in range(0, width, LANES):
        lanes = slice(low, low + LANES)
        picked = jnp.zeros((near_rows, LANES), F32)
        for step in range(CENTER_DILATION):
            strided = pl.ds(step, near_rows, stride=CENTER_DILATION)
            picked = jnp.where(center_ref[0:1, lanes] == step, spread_ref[low // LANES, strided, :], picked)
        near_ref[:, at0 + low : at0 + low + LANES] = picked.astype(BF16)


def first_forward_kernel(
    group, heads, valid_ref, table_ref, k_ref, q_ref, v_ref, g_ref, lanes_ref, after_ref,
    near_ref, qt_ref, gt_ref, kt_ref, vt_ref, *refs,
):
    *outs, spread_ref = refs
    select_near(lanes_ref, k_ref, near_ref, 0, spread_ref.at[0])
    select_near(lanes_ref, v_ref, near_ref, v_ref.shape[1], spread_ref.at[1])
    qt_ref[...] = q_ref[...].T
    vt_ref[...] = v_ref[...].T
    forward_heads(group, heads, valid_ref, table_ref, k_ref, qt_ref, vt_ref, *outs)
    gt_ref[...] = g_ref[...].T
    kt_ref[...] = k_ref[...].T


def forward_kernel(group, heads, valid_ref, table_ref, k_ref, qt_ref, vt_ref, after_ref, *outs):
    forward_heads(group, heads, valid_ref, table_ref, k_ref, qt_ref, vt_ref, *outs)


def stacks(heads, count):
    size = max(1, min(heads, STACK // count))
    found = []
    for first in range(0, heads, size):
        last = min(first + size, heads)
        found.append((first, last, window(first)[0], window(last - 1)[1]))
    return found


def head_lanes(h, low, high):
    lane = low + lax.broadcasted_iota(jnp.int32, (1, high - low), 1)
    return (lane >= h * HEAD_WIDTH) & (lane < (h + 1) * HEAD_WIDTH)


def stacked(rows, stack):
    first, last, low, high = stack
    return jnp.concatenate(
        [rows[:, low:high] * head_lanes(h, low, high).astype(F32).astype(BF16) for h in range(first, last)],
        axis=0,
    )


def unstack(ref, at0, stack, count, value, by, started):
    first, last, low, high = stack
    total = None
    for at, h in enumerate(range(first, last)):
        part = jnp.where(head_lanes(h, low, high), value[at * count : (at + 1) * count], 0.0)
        total = part if total is None else total + part
    total = total * by
    for at in range(low, high, LANES):
        part = total[:, at - low : at - low + LANES]
        if (at0, at) in started:
            ref[:, at0 + at : at0 + at + LANES] += part
        else:
            started.add((at0, at))
            ref[:, at0 + at : at0 + at + LANES] = part


def widen(value, rows):
    return jnp.concatenate([value] * (rows // LANES), axis=1)


def near_forward_kernel(heads, groups, valid_ref, table_ref, near_ref, qt_ref, *refs):
    parts = len(groups)
    o1_refs, max_refs, sum_refs = (refs[i * parts : (i + 1) * parts] for i in range(3))
    after_ref, p_ref, o_ref, old_ref, top_ref, sum_ref = refs[3 * parts :]
    width, rows = qt_ref.shape
    count = near_ref.shape[0]
    device = lax.axis_index(("seq", "sub"))
    row = lax.broadcasted_iota(jnp.int32, (count, LANES), 0)
    room = valid_ref[0] - ((device ^ 1) * rows + row * CENTER_DILATION)
    where = {}
    for part, (first, last) in enumerate(groups):
        for h in range(first, last):
            where[h] = part, h - first
    for stack in stacks(heads, count):
        first, last, low, high = stack
        scores = nn(stacked(near_ref[:, :width], stack), qt_ref[low:high, :])
        lifts, keeps = [], []
        for at, h in enumerate(range(first, last)):
            part, index = where[h]
            dead = jnp.where(table_ref[h : h + 1, :LANES] < room, 0.0, DEAD)
            here = scores[at * count : (at + 1) * count] + widen(dead, rows)
            old = max_refs[part][index : index + 1, :]
            top = jnp.maximum(jnp.max(here, axis=0, keepdims=True), old)
            lifted = jnp.exp2((here - top) * EXP2_SCALE)
            keep = jnp.exp2((old - top) * EXP2_SCALE)
            old_ref[h : h + 1, :] = old
            top_ref[h : h + 1, :] = top
            sum_ref[h : h + 1, :] = sum_refs[part][index : index + 1, :] * keep + jnp.sum(
                lifted, axis=0, keepdims=True
            )
            keeps.append(keep)
            lifts.append(lifted.astype(BF16))
        weights = jnp.concatenate(lifts, axis=0)
        p_ref[first * count : last * count, :] = weights
        added = nn(stacked(near_ref[:, width:], stack).T, weights)
        for keep, h in zip(keeps, range(first, last)):
            part, index = where[h]
            inside = added[h * HEAD_WIDTH - low : (h + 1) * HEAD_WIDTH - low]
            o_ref[head_rows(h), :] = o1_refs[part][head_rows(index), :] * keep + inside


def wide_kernel(
    heads, far_own, valid_ref, table_ref, far_ref, qt_ref, gt_ref, o_ref, old_ref, near_top_ref, near_sum_ref,
    ot_ref, local_ref, near_ref, delta_ref, ds_ref, keep_ref, send_ref, sum_ref,
):
    width, rows = qt_ref.shape
    count = far_ref.shape[0]
    half = count // 2
    device = lax.axis_index(("seq", "sub"))
    row = lax.broadcasted_iota(jnp.int32, (count, LANES), 0)
    slot = lax.shift_right_arithmetic(row, far_own.bit_length() - 1)
    place = (device ^ slot) * rows + (row & (far_own - 1)) * WIDE_DILATION
    room = jnp.where(slot == 0, -1, valid_ref[0] - place)
    started = set()
    for stack in stacks(heads, count):
        first, last, low, high = stack
        value_rows = stacked(far_ref[:, width:], stack)
        scores = nn(stacked(far_ref[:, :width], stack), qt_ref[low:high, :])
        grad_prob = nn(value_rows, gt_ref[low:high, :])
        probs, factors = [], []
        for at, h in enumerate(range(first, last)):
            one = slice(h, h + 1)
            dead = jnp.where(table_ref[heads + h : heads + h + 1, :LANES] < room, 0.0, DEAD)
            here = scores[at * count : (at + 1) * count] + widen(dead, rows)
            near_top = near_top_ref[one, :]
            top = jnp.maximum(jnp.max(here, axis=0, keepdims=True), near_top)
            lifted = jnp.exp2((here - top) * EXP2_SCALE)
            keep = jnp.exp2((near_top - top) * EXP2_SCALE)
            inverse = 1.0 / (near_sum_ref[one, :] * keep + jnp.sum(lifted, axis=0, keepdims=True))
            probs.append(lifted * inverse)
            factors.append(keep * inverse)
            near_ref[one, :] = keep * inverse
            local_ref[one, :] = jnp.exp2((old_ref[one, :] - top) * EXP2_SCALE) * inverse
        weights = jnp.concatenate([prob.astype(BF16) for prob in probs], axis=0)
        added = nn(value_rows.T, weights)
        dscores = []
        for at, h in enumerate(range(first, last)):
            inside = added[h * HEAD_WIDTH - low : (h + 1) * HEAD_WIDTH - low]
            context = o_ref[head_rows(h), :] * factors[at] + inside
            ot_ref[head_rows(h), :] = context.astype(BF16)
            delta = jnp.sum(gt_ref[head_rows(h), :].astype(F32) * context, axis=0, keepdims=True)
            delta_ref[h : h + 1, :] = delta
            here = grad_prob[at * count : (at + 1) * count]
            dscores.append((probs[at] * (here - delta)).astype(BF16))
        dscore = jnp.concatenate(dscores, axis=0)
        ds_ref[first * count : last * count, :] = dscore
        unstack(sum_ref, 0, stack, count, nt(dscore, qt_ref[low:high, :]), SCALE, started)
        unstack(sum_ref, width, stack, count, nt(weights, gt_ref[low:high, :]), 1.0, started)
    keep_ref[...] = sum_ref[:half, :]
    send_ref[...] = sum_ref[half:, :].astype(send_ref.dtype)


def near_backward_kernel(
    heads, near_ref, far_ref, qt_ref, gt_ref, p_ref, ds_ref, factor_ref, delta_ref, after_ref,
    dq_ref, send_ref, sum_ref,
):
    width, rows = qt_ref.shape
    count = near_ref.shape[0]
    started, begun = set(), set()

    def add_dq(stack, product):
        first, last, low, _ = stack
        for h in range(first, last):
            inside = product[h * HEAD_WIDTH - low : (h + 1) * HEAD_WIDTH - low]
            if h in begun:
                dq_ref[head_rows(h), :] += inside
            else:
                begun.add(h)
                dq_ref[head_rows(h), :] = inside

    for stack in stacks(heads, count):
        first, last, low, high = stack
        grad_prob = nn(stacked(near_ref[:, width:], stack), gt_ref[low:high, :])
        weights, dscores = [], []
        for at, h in enumerate(range(first, last)):
            prob = p_ref[h * count : (h + 1) * count, :].astype(F32) * factor_ref[h : h + 1, :]
            here = grad_prob[at * count : (at + 1) * count]
            weights.append(prob.astype(BF16))
            dscores.append((prob * (here - delta_ref[h : h + 1, :])).astype(BF16))
        dscore = jnp.concatenate(dscores, axis=0)
        add_dq(stack, nn(stacked(near_ref[:, :width], stack).T, dscore))
        unstack(sum_ref, 0, stack, count, nt(dscore, qt_ref[low:high, :]), SCALE, started)
        weight = jnp.concatenate(weights, axis=0)
        unstack(sum_ref, width, stack, count, nt(weight, gt_ref[low:high, :]), 1.0, started)
    send_ref[...] = sum_ref[...].astype(send_ref.dtype)
    count = far_ref.shape[0]
    for stack in stacks(heads, count):
        first, last, _, _ = stack
        dscore = ds_ref[first * count : last * count, :]
        add_dq(stack, nn(stacked(far_ref[:, :width], stack).T, dscore))


def backward_heads(
    group, p_ref, qt_ref, gt_ref, kt_ref, v_ref, dq2_ref, factor_ref, delta_ref, dqt_ref, dk_ref, dv_ref
):
    first, last = group
    rows = v_ref.shape[0]
    parts = [slice(at, at + rows // 2) for at in (0, rows // 2)]
    work = [(h, part) for h in range(first, last) for part in parts]

    def product(h, part):
        low, high = window(h)
        return nn(v_ref[part, low:high], embed(gt_ref[head_rows(h), :], h))

    following = product(*work[0])
    for index, (h, part) in enumerate(work):
        grad_prob = following
        if index + 1 < len(work):
            following = product(*work[index + 1])
        at, head = h - first, head_rows(h)
        here = head_rows(at)
        prob = p_ref[at, part, :].astype(F32) * factor_ref[h : h + 1, :]
        dv_ref[here, part] = nt(gt_ref[head, :], prob.astype(BF16))
        dscore = (prob * (grad_prob - delta_ref[h : h + 1, :])).astype(BF16)
        dk_ref[here, part] = nt(qt_ref[head, :], dscore)
        term = nn(kt_ref[head, part], dscore)
        dqt = term + (dq2_ref[head, :] if part is parts[0] else dqt)
        if part is parts[1]:
            dqt_ref[here, :] = (dqt * SCALE).astype(BF16)


def backward_kernel(group, *refs):
    backward_heads(group, *refs[:8], *refs[9:])


def turning_backward_kernel(group, *refs):
    ot_ref, out_ref = refs[9:11]
    backward_heads(group, *refs[:8], *refs[11:])
    out_ref[...] = ot_ref[...].T


def last_backward_kernel(groups, index, *refs):
    others = len(groups) - 1
    lanes_ref, back_ref, after_ref = refs[8:11]
    terms = refs[11 : 11 + 3 * others]
    dq_ref, sum_ref, dqt_ref, dk_ref, dv_ref, turned_ref, wide_ref = refs[11 + 3 * others :]
    backward_heads(groups[index], *refs[:8], dqt_ref, dk_ref, dv_ref)

    def all_groups(at, mine):
        found = list(terms[at * others : (at + 1) * others])
        found.insert(index, mine)
        return found

    rows, width = dq_ref.shape
    near_rows = rows // CENTER_DILATION
    for (first, last), ref in zip(groups, all_groups(0, dqt_ref)):
        turned_ref[first * HEAD_WIDTH : last * HEAD_WIDTH, :] = ref[...]
    dq_ref[...] = turned_ref[...].T
    for at, parts, by in ((0, all_groups(1, dk_ref), SCALE), (width, all_groups(2, dv_ref), 1.0)):
        for (first, last), ref in zip(groups, parts):
            wide_ref[first * HEAD_WIDTH : last * HEAD_WIDTH, :] = ref[...] * by
        for low in range(0, width, LANES):
            block = (at + low) // LANES
            sum_ref[block] = wide_ref[low : low + LANES, :].T
            near = back_ref[:, at + low : at + low + LANES].astype(F32)
            center = lanes_ref[0:1, low : low + LANES]
            for step in range(CENTER_DILATION):
                strided = pl.ds(step, near_rows, stride=CENTER_DILATION)
                sum_ref[block, strided, :] += jnp.where(center == step, near, 0.0)


def combine_kernel(lanes_ref, sum_ref, far_ref, outk_ref, outv_ref):
    rows, width = outk_ref.shape
    far_rows = far_ref.shape[0]
    row = lax.broadcasted_iota(jnp.int32, (WIDE_DILATION, LANES), 0)
    for at, out in ((0, outk_ref), (width, outv_ref)):
        for low in range(0, width, LANES):
            block = (at + low) // LANES
            mask = row == lanes_ref[1:2, low : low + LANES]
            for index in range(far_rows):
                part = slice(index * WIDE_DILATION, (index + 1) * WIDE_DILATION)
                far = far_ref[index : index + 1, at + low : at + low + LANES]
                value = sum_ref[block, part, :] + jnp.where(mask, far, 0.0)
                out[part, low : low + LANES] = value.astype(BF16)


ANY = pl.BlockSpec(memory_space=pl.ANY)
HBM = pl.BlockSpec(memory_space=pltpu.HBM)


def call(body, outs, ins, scratch=(), *, flops=0, moved=0):
    return pl.pallas_call(
        body,
        out_shape=[jax.ShapeDtypeStruct(s, d) for s, d in outs],
        in_specs=ins,
        out_specs=[VMEM] * len(outs),
        scratch_shapes=list(scratch),
        compiler_params=pltpu.CompilerParams(vmem_limit_bytes=24 * 2**20),
        cost_estimate=pl.CostEstimate(flops=flops, bytes_accessed=moved, transcendentals=0),
    )


def local(queries, keys, values, grad_out, center_shift, wide_shift, valid_count):
    rows, width = queries.shape
    heads = width // HEAD_WIDTH
    groups = head_groups(heads)
    near_rows, far_own = rows // CENTER_DILATION, rows // WIDE_DILATION
    axes = ("seq", "sub")
    devices = lax.axis_size(axes)
    far_rows = far_own * devices
    blocks = 2 * width // LANES
    steps = [2**bit for bit in range(devices.bit_length() - 1)]

    def swap(value, apart):
        return lax.ppermute(value, axes, [(at, at ^ apart) for at in range(devices)])

    far, q, k, v, g, table, lanes = call(
        functools.partial(select_kernel, heads),
        [((far_own, 2 * width), BF16)]
        + [((rows, width), BF16)] * 4
        + [((2 * heads, rows), jnp.int32), ((8, width), jnp.int32)],
        [HBM] * 6,
        [
            pltpu.SMEM(center_shift.shape, jnp.int32),
            pltpu.SMEM(wide_shift.shape, jnp.int32),
            pltpu.SemaphoreType.DMA((6,)),
        ],
        moved=16 * rows * width,
    )(
        *(
            pltpu.with_memory_space_constraint(value, pltpu.HBM)
            for value in (center_shift, wide_shift, queries, keys, values, grad_out)
        )
    )

    valid, far = lax.optimization_barrier((valid_count, far))

    def cost(heads_done, keys_done, products):
        done = heads_done * keys_done * rows
        return dict(flops=2 * HEAD_WIDTH * done * products * 5, moved=2 * done)

    turned = {}
    fronts = {}

    def front(index, after):
        first, last = groups[index]
        size, tall = last - first, (last - first) * HEAD_WIDTH
        outs = [((size, rows, rows), BF16), ((tall, rows), F32), ((size, rows), F32), ((size, rows), F32)]
        if not turned:
            *flipped, p, o, top, total = call(
                functools.partial(first_forward_kernel, groups[index], heads),
                [((near_rows, 2 * width), BF16)] + [((width, rows), BF16)] * 4 + outs,
                [SMEM] + [VMEM] * 6 + [ANY],
                [pltpu.VMEM((2, blocks // 2, rows, LANES), F32)],
                **cost(size, rows, 2),
            )(valid, table, k, q, v, g, lanes, after)
            turned.update(zip(("near", "qt", "gt", "kt", "vt"), flipped))
        else:
            p, o, top, total = call(
                functools.partial(forward_kernel, groups[index], heads),
                outs,
                [SMEM] + [VMEM] * 4 + [ANY],
                **cost(size, rows, 2),
            )(valid, table, k, turned["qt"], turned["vt"], after)
        fronts[index] = [p, o, top, total]

    def tie(arrived, holder, key):
        arrived, held = lax.optimization_barrier((arrived, holder[key][-1]))
        holder[key] = [*holder[key][:-1], held]
        return arrived

    last = len(groups) - 1
    front_order, back_order = [last, *range(last)], [*range(last, -1, -1)]
    after = far
    for at, step in enumerate(steps):
        if at == 1:
            near_out, far = lax.optimization_barrier((turned["near"], far))
        arrived = swap(far, step)
        if at == 1:
            near_came = swap(near_out, 1)
        if at < len(groups):
            front(front_order[at], after)
        if at == len(groups) - 1:
            p, o, top, total = zip(*(fronts[index] for index in range(len(groups))))
            fronts["near"] = call(
                functools.partial(near_forward_kernel, heads, groups),
                [((heads * near_rows, rows), BF16), ((width, rows), F32)] + [((heads, rows), F32)] * 3,
                [SMEM] + [VMEM] * (3 + 3 * len(groups)) + [ANY],
                **cost(heads, near_rows, 2),
            )(valid, table, near_came, turned["qt"], *o, *top, *total, after)
            arrived = tie(arrived, fronts, "near")
        elif at < len(groups):
            arrived = tie(arrived, fronts, front_order[at])
        after = arrived
        far = jnp.concatenate([far, arrived], axis=0)
    near_p, o, old, near_top, near_sum = fronts["near"]
    qt, gt, kt = (turned[name] for name in ("qt", "gt", "kt"))

    ot, local_factor, near_factor, delta, ds, terms, send = call(
        functools.partial(wide_kernel, heads, far_own),
        [((width, rows), BF16)]
        + [((heads, rows), F32)] * 3
        + [((heads * far_rows, rows), BF16)]
        + [((far_rows // 2, 2 * width), F32)] * 2,
        [SMEM] + [VMEM] * 8,
        [pltpu.VMEM((far_rows, 2 * width), F32)],
        **cost(heads, far_rows, 5),
    )(valid, table, far, qt, gt, o, old, near_top, near_sum)

    backs = {}

    def back(index, after):
        first, end = groups[index]
        size, tall = end - first, (end - first) * HEAD_WIDTH
        partial = [((tall, rows), BF16), ((tall, rows), F32), ((tall, rows), F32)]
        given = (p[index], qt, gt, kt, v, backs["near"][0], local_factor, delta)
        if len(backs) == OUT_AT:
            backs["out"], *backs[index] = call(
                functools.partial(turning_backward_kernel, groups[index]),
                [((rows, width), BF16), *partial],
                [VMEM] * 8 + [ANY, VMEM],
                **cost(size, rows, 4),
            )(*given, after, ot)
            return
        if len(backs) < len(groups):
            backs[index] = call(
                functools.partial(backward_kernel, groups[index]),
                partial,
                [VMEM] * 8 + [ANY],
                **cost(size, rows, 4),
            )(*given, after)
            return
        others = [backs[other] for other in range(len(groups)) if other != index]
        backs[index] = call(
            functools.partial(last_backward_kernel, groups, index),
            [((rows, width), BF16), ((blocks, rows, LANES), F32)],
            [VMEM] * 10 + [ANY] + [VMEM] * (3 * len(others)),
            [pltpu.VMEM(shape, dtype) for shape, dtype in partial]
            + [pltpu.VMEM((width, rows), BF16), pltpu.VMEM((width, rows), F32)],
            **cost(size, rows, 4),
        )(*given, lanes, near_back, after, *[terms[i] for i in range(3) for terms in others])

    after = send
    for at, step in enumerate(reversed(steps)):
        if at:
            half = terms.shape[0] // 2
            send, terms = terms[half:], terms[:half]
        arrived = swap(send, step)
        if at == 0:
            backs["near"] = call(
                functools.partial(near_backward_kernel, heads),
                [((width, rows), F32), ((near_rows, 2 * width), BF16)],
                [VMEM] * 8 + [ANY],
                [pltpu.VMEM((near_rows, 2 * width), F32)],
                **cost(heads, near_rows, 4),
            )(near_came, far, qt, gt, near_p, ds, near_factor, delta, after)
        if at == 1:
            near_back = swap(backs["near"][1], 1)
        if at < len(groups):
            back(back_order[at], after)
            arrived = tie(arrived, backs, back_order[at])
        after = arrived
        terms = terms + arrived.astype(F32)

    dq, sums = backs[back_order[-1]]
    key_gradient, value_gradient = call(
        combine_kernel,
        [((rows, width), BF16)] * 2,
        [VMEM] * 3,
        moved=12 * rows * width,
    )(lanes, sums, terms)
    return backs["out"], dq, key_gradient, value_gradient


def solution(mesh):
    split = P(("grp", "seq", "sub"), "hd")
    return jax.shard_map(
        local,
        mesh=mesh,
        in_specs=(split, split, split, split, P(), P(), P("grp")),
        out_specs=(split, split, split, split),
        check_vma=False,
    )
```

```python
import functools
import math

import jax
import jax.numpy as jnp
from jax import lax
from jax.experimental import pallas as pl
from jax.experimental.pallas import tpu as pltpu
from jax.sharding import PartitionSpec as P

HEAD_WIDTH = 48
CENTER_DILATION = 8
WIDE_DILATION = 128
LANES = 128
STACK = 256
ONES = 16
OUT_AT = 2
DEAD = -1e30
SCALE = HEAD_WIDTH**-0.5
EXP2_SCALE = SCALE * math.log2(math.e)
F32 = jnp.float32
BF16 = jnp.bfloat16

VMEM = pl.BlockSpec(memory_space=pltpu.VMEM)
SMEM = pl.BlockSpec(memory_space=pltpu.SMEM)


def nn(a, b):
    return jnp.dot(a, b, preferred_element_type=F32)


def nt(a, b):
    return lax.dot_general(a, b, (((1,), (1,)), ((), ())), preferred_element_type=F32)


def head_rows(h):
    return slice(h * HEAD_WIDTH, (h + 1) * HEAD_WIDTH)


def window(h):
    low = h * HEAD_WIDTH // LANES * LANES
    high = -(-(h + 1) * HEAD_WIDTH // LANES) * LANES
    return low, high


def embed(rows, h):
    low, high = window(h)
    before, after = h * HEAD_WIDTH - low, high - (h + 1) * HEAD_WIDTH
    parts = [rows]
    if before:
        parts.insert(0, jnp.zeros((before, rows.shape[1]), rows.dtype))
    if after:
        parts.append(jnp.zeros((after, rows.shape[1]), rows.dtype))
    return jnp.concatenate(parts, axis=0) if len(parts) > 1 else rows


def head_groups(heads):
    edge = max(1, heads // 4)
    return [(0, edge), (edge, heads - edge), (heads - edge, heads)]


def lane_shifts(shift_ref, base, heads, width):
    lane = lax.broadcasted_iota(jnp.int32, (1, width), 1)
    row = jnp.zeros((1, width), jnp.int32)
    for h in range(heads):
        inside = (lane >= h * HEAD_WIDTH) & (lane < (h + 1) * HEAD_WIDTH)
        row = jnp.where(inside, shift_ref[base + h], row)
    return row


def head_base(heads):
    return lax.axis_index("hd") * heads


def select_kernel(
    heads, center_any, wide_any, q_any, k_any, v_any, g_any,
    far_ref, q_ref, k_ref, v_ref, g_ref, table_ref, lanes_ref,
    center_ref, wide_ref, sems,
):
    rows, width = k_ref.shape
    pairs = (
        (center_any, center_ref), (wide_any, wide_ref),
        (k_any, k_ref), (v_any, v_ref), (q_any, q_ref), (g_any, g_ref),
    )
    copies = [pltpu.make_async_copy(a, b, sems.at[i]) for i, (a, b) in enumerate(pairs)]
    for copy in copies:
        copy.start()
    for copy in copies[:2]:
        copy.wait()
    base = head_base(heads)
    center = lane_shifts(center_ref, base, heads, width)
    wide = lane_shifts(wide_ref, base, heads, width)
    lanes_ref[0:1, :] = center
    lanes_ref[1:2, :] = wide
    for h in range(heads):
        table_ref[h : h + 1, :] = jnp.full((1, rows), center_ref[base + h], jnp.int32)
        table_ref[heads + h : heads + h + 1, :] = jnp.full((1, rows), wide_ref[base + h], jnp.int32)
    far_rows = rows // WIDE_DILATION
    row = lax.broadcasted_iota(jnp.int32, (far_rows, WIDE_DILATION, LANES), 1)
    for at, ref, copy in ((0, k_ref, copies[2]), (width, v_ref, copies[3])):
        copy.wait()
        for low in range(0, width, LANES):
            lanes = slice(low, low + LANES)
            packed = slice(at + low, at + low + LANES)
            spread = ref[:, lanes].astype(F32)
            chosen = jnp.where(row == wide[:, lanes], spread.reshape(row.shape), 0.0)
            far_ref[:, packed] = jnp.sum(chosen, axis=1).astype(BF16)
    copies[4].wait()
    copies[5].wait()


def forward_heads(
    group, heads, valid_ref, table_ref, k_ref, qt_ref, vt_ref, p_ref, ot_ref, max_ref, sum_ref
):
    first, last = group
    rows = k_ref.shape[0]
    device = lax.axis_index(("seq", "sub"))
    row = lax.broadcasted_iota(jnp.int32, (rows, LANES), 0)
    dead = jnp.where(device * rows + row < valid_ref[0], 0.0, DEAD)
    ones = jnp.ones((ONES, rows), BF16)

    def scores_of(h):
        low, high = window(h)
        is_near = (row & (CENTER_DILATION - 1)) == table_ref[h : h + 1, :LANES]
        is_far = (row & (WIDE_DILATION - 1)) == table_ref[heads + h : heads + h + 1, :LANES]
        once = jnp.where(is_near | is_far, 1.0 / EXP2_SCALE, 0.0)
        bias = dead + jnp.where(is_near & is_far, math.log2(3) / EXP2_SCALE, once)
        scores = nn(k_ref[:, low:high], embed(qt_ref[head_rows(h), :], h)) + widen(bias, rows)
        return scores, jnp.max(scores, axis=0, keepdims=True)

    following = scores_of(first)
    for h in range(first, last):
        scores, top = following
        if h + 1 < last:
            following = scores_of(h + 1)
        at = h - first
        weights = jnp.exp2((scores - top) * EXP2_SCALE).astype(BF16)
        p_ref[at] = weights
        summed = nn(jnp.concatenate([vt_ref[head_rows(h), :], ones], axis=0), weights)
        max_ref[at : at + 1, :] = top
        sum_ref[at : at + 1, :] = summed[HEAD_WIDTH : HEAD_WIDTH + 1]
        ot_ref[head_rows(at), :] = summed[:HEAD_WIDTH]


def select_near(center_ref, source_ref, near_ref, at0, spread_ref):
    rows, width = source_ref.shape
    near_rows = rows // CENTER_DILATION
    for low in range(0, width, LANES):
        lanes = slice(low, low + LANES)
        spread_ref[low // LANES] = source_ref[:, lanes].astype(F32)
    for low in range(0, width, LANES):
        lanes = slice(low, low + LANES)
        picked = jnp.zeros((near_rows, LANES), F32)
        for step in range(CENTER_DILATION):
            strided = pl.ds(step, near_rows, stride=CENTER_DILATION)
            picked = jnp.where(center_ref[0:1, lanes] == step, spread_ref[low // LANES, strided, :], picked)
        near_ref[:, at0 + low : at0 + low + LANES] = picked.astype(BF16)


def first_forward_kernel(
    group, heads, valid_ref, table_ref, k_ref, q_ref, v_ref, g_ref, lanes_ref, after_ref,
    near_ref, qt_ref, gt_ref, kt_ref, vt_ref, *refs,
):
    *outs, spread_ref = refs
    select_near(lanes_ref, k_ref, near_ref, 0, spread_ref.at[0])
    select_near(lanes_ref, v_ref, near_ref, v_ref.shape[1], spread_ref.at[1])
    qt_ref[...] = q_ref[...].T
    vt_ref[...] = v_ref[...].T
    forward_heads(group, heads, valid_ref, table_ref, k_ref, qt_ref, vt_ref, *outs)
    gt_ref[...] = g_ref[...].T
    kt_ref[...] = k_ref[...].T


def forward_kernel(group, heads, valid_ref, table_ref, k_ref, qt_ref, vt_ref, after_ref, *outs):
    forward_heads(group, heads, valid_ref, table_ref, k_ref, qt_ref, vt_ref, *outs)


def stacks(heads, count):
    size = max(1, min(heads, STACK // count))
    found = []
    for first in range(0, heads, size):
        last = min(first + size, heads)
        found.append((first, last, window(first)[0], window(last - 1)[1]))
    return found


def head_lanes(h, low, high):
    lane = low + lax.broadcasted_iota(jnp.int32, (1, high - low), 1)
    return (lane >= h * HEAD_WIDTH) & (lane < (h + 1) * HEAD_WIDTH)


def stacked(rows, stack):
    first, last, low, high = stack
    return jnp.concatenate(
        [rows[:, low:high] * head_lanes(h, low, high).astype(F32).astype(BF16) for h in range(first, last)],
        axis=0,
    )


def unstack(ref, at0, stack, count, value, by, started):
    first, last, low, high = stack
    total = None
    for at, h in enumerate(range(first, last)):
        part = jnp.where(head_lanes(h, low, high), value[at * count : (at + 1) * count], 0.0)
        total = part if total is None else total + part
    total = total * by
    for at in range(low, high, LANES):
        part = total[:, at - low : at - low + LANES]
        if (at0, at) in started:
            ref[:, at0 + at : at0 + at + LANES] += part
        else:
            started.add((at0, at))
            ref[:, at0 + at : at0 + at + LANES] = part


def widen(value, rows):
    return jnp.concatenate([value] * (rows // LANES), axis=1)


def near_forward_kernel(heads, groups, valid_ref, table_ref, near_ref, qt_ref, *refs):
    parts = len(groups)
    o1_refs, max_refs, sum_refs = (refs[i * parts : (i + 1) * parts] for i in range(3))
    after_ref, p_ref, o_ref, old_ref, top_ref, sum_ref = refs[3 * parts :]
    width, rows = qt_ref.shape
    count = near_ref.shape[0]
    device = lax.axis_index(("seq", "sub"))
    row = lax.broadcasted_iota(jnp.int32, (count, LANES), 0)
    room = valid_ref[0] - ((device ^ 1) * rows + row * CENTER_DILATION)
    where = {}
    for part, (first, last) in enumerate(groups):
        for h in range(first, last):
            where[h] = part, h - first
    for stack in stacks(heads, count):
        first, last, low, high = stack
        scores = nn(stacked(near_ref[:, :width], stack), qt_ref[low:high, :])
        lifts, keeps = [], []
        for at, h in enumerate(range(first, last)):
            part, index = where[h]
            dead = jnp.where(table_ref[h : h + 1, :LANES] < room, 0.0, DEAD)
            here = scores[at * count : (at + 1) * count] + widen(dead, rows)
            old = max_refs[part][index : index + 1, :]
            top = jnp.maximum(jnp.max(here, axis=0, keepdims=True), old)
            lifted = jnp.exp2((here - top) * EXP2_SCALE)
            keep = jnp.exp2((old - top) * EXP2_SCALE)
            old_ref[h : h + 1, :] = old
            top_ref[h : h + 1, :] = top
            sum_ref[h : h + 1, :] = sum_refs[part][index : index + 1, :] * keep + jnp.sum(
                lifted, axis=0, keepdims=True
            )
            keeps.append(keep)
            lifts.append(lifted.astype(BF16))
        weights = jnp.concatenate(lifts, axis=0)
        p_ref[first * count : last * count, :] = weights
        added = nn(stacked(near_ref[:, width:], stack).T, weights)
        for keep, h in zip(keeps, range(first, last)):
            part, index = where[h]
            inside = added[h * HEAD_WIDTH - low : (h + 1) * HEAD_WIDTH - low]
            o_ref[head_rows(h), :] = o1_refs[part][head_rows(index), :] * keep + inside


def wide_kernel(
    heads, far_own, valid_ref, table_ref, far_ref, qt_ref, gt_ref, o_ref, old_ref, near_top_ref, near_sum_ref,
    ot_ref, local_ref, near_ref, delta_ref, ds_ref, keep_ref, send_ref, sum_ref,
):
    width, rows = qt_ref.shape
    count = far_ref.shape[0]
    half = count // 2
    device = lax.axis_index(("seq", "sub"))
    row = lax.broadcasted_iota(jnp.int32, (count, LANES), 0)
    slot = lax.shift_right_arithmetic(row, far_own.bit_length() - 1)
    place = (device ^ slot) * rows + (row & (far_own - 1)) * WIDE_DILATION
    room = jnp.where(slot == 0, -1, valid_ref[0] - place)
    started = set()
    for stack in stacks(heads, count):
        first, last, low, high = stack
        value_rows = stacked(far_ref[:, width:], stack)
        scores = nn(stacked(far_ref[:, :width], stack), qt_ref[low:high, :])
        grad_prob = nn(value_rows, gt_ref[low:high, :])
        probs, factors = [], []
        for at, h in enumerate(range(first, last)):
            one = slice(h, h + 1)
            dead = jnp.where(table_ref[heads + h : heads + h + 1, :LANES] < room, 0.0, DEAD)
            here = scores[at * count : (at + 1) * count] + widen(dead, rows)
            near_top = near_top_ref[one, :]
            top = jnp.maximum(jnp.max(here, axis=0, keepdims=True), near_top)
            lifted = jnp.exp2((here - top) * EXP2_SCALE)
            keep = jnp.exp2((near_top - top) * EXP2_SCALE)
            inverse = 1.0 / (near_sum_ref[one, :] * keep + jnp.sum(lifted, axis=0, keepdims=True))
            probs.append(lifted * inverse)
            factors.append(keep * inverse)
            near_ref[one, :] = keep * inverse
            local_ref[one, :] = jnp.exp2((old_ref[one, :] - top) * EXP2_SCALE) * inverse
        weights = jnp.concatenate([prob.astype(BF16) for prob in probs], axis=0)
        added = nn(value_rows.T, weights)
        dscores = []
        for at, h in enumerate(range(first, last)):
            inside = added[h * HEAD_WIDTH - low : (h + 1) * HEAD_WIDTH - low]
            context = o_ref[head_rows(h), :] * factors[at] + inside
            ot_ref[head_rows(h), :] = context.astype(BF16)
            delta = jnp.sum(gt_ref[head_rows(h), :].astype(F32) * context, axis=0, keepdims=True)
            delta_ref[h : h + 1, :] = delta
            here = grad_prob[at * count : (at + 1) * count]
            dscores.append((probs[at] * (here - delta)).astype(BF16))
        dscore = jnp.concatenate(dscores, axis=0)
        ds_ref[first * count : last * count, :] = dscore
        unstack(sum_ref, 0, stack, count, nt(dscore, qt_ref[low:high, :]), SCALE, started)
        unstack(sum_ref, width, stack, count, nt(weights, gt_ref[low:high, :]), 1.0, started)
    keep_ref[...] = sum_ref[:half, :]
    send_ref[...] = sum_ref[half:, :].astype(send_ref.dtype)


def near_backward_kernel(
    heads, near_ref, far_ref, qt_ref, gt_ref, p_ref, ds_ref, factor_ref, delta_ref, after_ref,
    dq_ref, send_ref, sum_ref,
):
    width, rows = qt_ref.shape
    count = near_ref.shape[0]
    started, begun = set(), set()

    def add_dq(stack, product):
        first, last, low, _ = stack
        for h in range(first, last):
            inside = product[h * HEAD_WIDTH - low : (h + 1) * HEAD_WIDTH - low]
            if h in begun:
                dq_ref[head_rows(h), :] += inside
            else:
                begun.add(h)
                dq_ref[head_rows(h), :] = inside

    for stack in stacks(heads, count):
        first, last, low, high = stack
        grad_prob = nn(stacked(near_ref[:, width:], stack), gt_ref[low:high, :])
        weights, dscores = [], []
        for at, h in enumerate(range(first, last)):
            prob = p_ref[h * count : (h + 1) * count, :].astype(F32) * factor_ref[h : h + 1, :]
            here = grad_prob[at * count : (at + 1) * count]
            weights.append(prob.astype(BF16))
            dscores.append((prob * (here - delta_ref[h : h + 1, :])).astype(BF16))
        dscore = jnp.concatenate(dscores, axis=0)
        add_dq(stack, nn(stacked(near_ref[:, :width], stack).T, dscore))
        unstack(sum_ref, 0, stack, count, nt(dscore, qt_ref[low:high, :]), SCALE, started)
        weight = jnp.concatenate(weights, axis=0)
        unstack(sum_ref, width, stack, count, nt(weight, gt_ref[low:high, :]), 1.0, started)
    send_ref[...] = sum_ref[...].astype(send_ref.dtype)
    count = far_ref.shape[0]
    for stack in stacks(heads, count):
        first, last, _, _ = stack
        dscore = ds_ref[first * count : last * count, :]
        add_dq(stack, nn(stacked(far_ref[:, :width], stack).T, dscore))


def backward_heads(
    group, p_ref, qt_ref, gt_ref, kt_ref, v_ref, dq2_ref, factor_ref, delta_ref, dqt_ref, dk_ref, dv_ref
):
    first, last = group
    rows = v_ref.shape[0]
    parts = [slice(at, at + rows // 2) for at in (0, rows // 2)]
    work = [(h, part) for h in range(first, last) for part in parts]

    def product(h, part):
        low, high = window(h)
        return nn(v_ref[part, low:high], embed(gt_ref[head_rows(h), :], h))

    following = product(*work[0])
    for index, (h, part) in enumerate(work):
        grad_prob = following
        if index + 1 < len(work):
            following = product(*work[index + 1])
        at, head = h - first, head_rows(h)
        here = head_rows(at)
        prob = p_ref[at, part, :].astype(F32) * factor_ref[h : h + 1, :]
        dv_ref[here, part] = nt(gt_ref[head, :], prob.astype(BF16))
        dscore = (prob * (grad_prob - delta_ref[h : h + 1, :])).astype(BF16)
        dk_ref[here, part] = nt(qt_ref[head, :], dscore)
        term = nn(kt_ref[head, part], dscore)
        dqt = term + (dq2_ref[head, :] if part is parts[0] else dqt)
        if part is parts[1]:
            dqt_ref[here, :] = (dqt * SCALE).astype(BF16)


def backward_kernel(group, *refs):
    backward_heads(group, *refs[:8], *refs[9:])


def turning_backward_kernel(group, *refs):
    ot_ref, out_ref = refs[9:11]
    backward_heads(group, *refs[:8], *refs[11:])
    out_ref[...] = ot_ref[...].T


def last_backward_kernel(groups, index, *refs):
    others = len(groups) - 1
    lanes_ref, back_ref, out_ref, after_ref = refs[8:12]
    terms = refs[12 : 12 + 3 * others]
    out_any, dq_any, sum_ref, dqt_ref, dk_ref, dv_ref, turned_ref, wide_ref, dq_ref, sems = refs[12 + 3 * others :]
    copies = [
        pltpu.make_async_copy(out_ref, out_any, sems.at[0]),
        pltpu.make_async_copy(dq_ref, dq_any, sems.at[1]),
    ]
    copies[0].start()
    backward_heads(groups[index], *refs[:8], dqt_ref, dk_ref, dv_ref)

    def all_groups(at, mine):
        found = list(terms[at * others : (at + 1) * others])
        found.insert(index, mine)
        return found

    rows, width = dq_ref.shape
    near_rows = rows // CENTER_DILATION
    for (first, last), ref in zip(groups, all_groups(0, dqt_ref)):
        turned_ref[first * HEAD_WIDTH : last * HEAD_WIDTH, :] = ref[...]
    dq_ref[...] = turned_ref[...].T
    copies[1].start()
    for at, parts, by in ((0, all_groups(1, dk_ref), SCALE), (width, all_groups(2, dv_ref), 1.0)):
        for (first, last), ref in zip(groups, parts):
            wide_ref[first * HEAD_WIDTH : last * HEAD_WIDTH, :] = ref[...] * by
        for low in range(0, width, LANES):
            block = (at + low) // LANES
            sum_ref[block] = wide_ref[low : low + LANES, :].T
            near = back_ref[:, at + low : at + low + LANES].astype(F32)
            center = lanes_ref[0:1, low : low + LANES]
            for step in range(CENTER_DILATION):
                strided = pl.ds(step, near_rows, stride=CENTER_DILATION)
                sum_ref[block, strided, :] += jnp.where(center == step, near, 0.0)
    for copy in copies:
        copy.wait()


def combine_kernel(lanes_ref, sum_ref, far_ref, outk_ref, outv_ref):
    rows, width = outk_ref.shape
    far_rows = far_ref.shape[0]
    row = lax.broadcasted_iota(jnp.int32, (WIDE_DILATION, LANES), 0)
    for at, out in ((0, outk_ref), (width, outv_ref)):
        for low in range(0, width, LANES):
            block = (at + low) // LANES
            mask = row == lanes_ref[1:2, low : low + LANES]
            for index in range(far_rows):
                part = slice(index * WIDE_DILATION, (index + 1) * WIDE_DILATION)
                far = far_ref[index : index + 1, at + low : at + low + LANES]
                value = sum_ref[block, part, :] + jnp.where(mask, far, 0.0)
                out[part, low : low + LANES] = value.astype(BF16)


ANY = pl.BlockSpec(memory_space=pl.ANY)
HBM = pl.BlockSpec(memory_space=pltpu.HBM)


def call(body, outs, ins, scratch=(), *, in_hbm=0, flops=0, moved=0):
    return pl.pallas_call(
        body,
        out_shape=[jax.ShapeDtypeStruct(s, d) for s, d in outs],
        in_specs=ins,
        out_specs=[HBM] * in_hbm + [VMEM] * (len(outs) - in_hbm),
        scratch_shapes=list(scratch),
        compiler_params=pltpu.CompilerParams(vmem_limit_bytes=24 * 2**20),
        cost_estimate=pl.CostEstimate(flops=flops, bytes_accessed=moved, transcendentals=0),
    )


def local(queries, keys, values, grad_out, center_shift, wide_shift, valid_count):
    rows, width = queries.shape
    heads = width // HEAD_WIDTH
    groups = head_groups(heads)
    near_rows, far_own = rows // CENTER_DILATION, rows // WIDE_DILATION
    axes = ("seq", "sub")
    devices = lax.axis_size(axes)
    far_rows = far_own * devices
    blocks = 2 * width // LANES
    steps = [2**bit for bit in range(devices.bit_length() - 1)]

    def swap(value, apart):
        return lax.ppermute(value, axes, [(at, at ^ apart) for at in range(devices)])

    far, q, k, v, g, table, lanes = call(
        functools.partial(select_kernel, heads),
        [((far_own, 2 * width), BF16)]
        + [((rows, width), BF16)] * 4
        + [((2 * heads, rows), jnp.int32), ((8, width), jnp.int32)],
        [HBM] * 6,
        [
            pltpu.SMEM(center_shift.shape, jnp.int32),
            pltpu.SMEM(wide_shift.shape, jnp.int32),
            pltpu.SemaphoreType.DMA((6,)),
        ],
        moved=16 * rows * width,
    )(
        *(
            pltpu.with_memory_space_constraint(value, pltpu.HBM)
            for value in (center_shift, wide_shift, queries, keys, values, grad_out)
        )
    )

    valid, far = lax.optimization_barrier((valid_count, far))

    def cost(heads_done, keys_done, products):
        done = heads_done * keys_done * rows
        return dict(flops=2 * HEAD_WIDTH * done * products * 5, moved=2 * done)

    turned = {}
    fronts = {}

    def front(index, after):
        first, last = groups[index]
        size, tall = last - first, (last - first) * HEAD_WIDTH
        outs = [((size, rows, rows), BF16), ((tall, rows), F32), ((size, rows), F32), ((size, rows), F32)]
        if not turned:
            *flipped, p, o, top, total = call(
                functools.partial(first_forward_kernel, groups[index], heads),
                [((near_rows, 2 * width), BF16)] + [((width, rows), BF16)] * 4 + outs,
                [SMEM] + [VMEM] * 6 + [ANY],
                [pltpu.VMEM((2, blocks // 2, rows, LANES), F32)],
                **cost(size, rows, 2),
            )(valid, table, k, q, v, g, lanes, after)
            turned.update(zip(("near", "qt", "gt", "kt", "vt"), flipped))
        else:
            p, o, top, total = call(
                functools.partial(forward_kernel, groups[index], heads),
                outs,
                [SMEM] + [VMEM] * 4 + [ANY],
                **cost(size, rows, 2),
            )(valid, table, k, turned["qt"], turned["vt"], after)
        fronts[index] = [p, o, top, total]

    def tie(arrived, holder, key):
        arrived, held = lax.optimization_barrier((arrived, holder[key][-1]))
        holder[key] = [*holder[key][:-1], held]
        return arrived

    last = len(groups) - 1
    front_order, back_order = [last, *range(last)], [*range(last, -1, -1)]
    after = far
    for at, step in enumerate(steps):
        if at == 1:
            near_out, far = lax.optimization_barrier((turned["near"], far))
        arrived = swap(far, step)
        if at == 1:
            near_came = swap(near_out, 1)
        if at < len(groups):
            front(front_order[at], after)
        if at == len(groups) - 1:
            p, o, top, total = zip(*(fronts[index] for index in range(len(groups))))
            fronts["near"] = call(
                functools.partial(near_forward_kernel, heads, groups),
                [((heads * near_rows, rows), BF16), ((width, rows), F32)] + [((heads, rows), F32)] * 3,
                [SMEM] + [VMEM] * (3 + 3 * len(groups)) + [ANY],
                **cost(heads, near_rows, 2),
            )(valid, table, near_came, turned["qt"], *o, *top, *total, after)
            arrived = tie(arrived, fronts, "near")
        elif at < len(groups):
            arrived = tie(arrived, fronts, front_order[at])
        after = arrived
        far = jnp.concatenate([far, arrived], axis=0)
    near_p, o, old, near_top, near_sum = fronts["near"]
    qt, gt, kt = (turned[name] for name in ("qt", "gt", "kt"))

    ot, local_factor, near_factor, delta, ds, terms, send = call(
        functools.partial(wide_kernel, heads, far_own),
        [((width, rows), BF16)]
        + [((heads, rows), F32)] * 3
        + [((heads * far_rows, rows), BF16)]
        + [((far_rows // 2, 2 * width), F32)] * 2,
        [SMEM] + [VMEM] * 8,
        [pltpu.VMEM((far_rows, 2 * width), F32)],
        **cost(heads, far_rows, 5),
    )(valid, table, far, qt, gt, o, old, near_top, near_sum)

    backs = {}

    def back(index, after):
        first, end = groups[index]
        size, tall = end - first, (end - first) * HEAD_WIDTH
        partial = [((tall, rows), BF16), ((tall, rows), F32), ((tall, rows), F32)]
        given = (p[index], qt, gt, kt, v, backs["near"][0], local_factor, delta)
        if len(backs) == OUT_AT:
            backs["out"], *backs[index] = call(
                functools.partial(turning_backward_kernel, groups[index]),
                [((rows, width), BF16), *partial],
                [VMEM] * 8 + [ANY, VMEM],
                **cost(size, rows, 4),
            )(*given, after, ot)
            return
        if len(backs) < len(groups):
            backs[index] = call(
                functools.partial(backward_kernel, groups[index]),
                partial,
                [VMEM] * 8 + [ANY],
                **cost(size, rows, 4),
            )(*given, after)
            return
        others = [backs[other] for other in range(len(groups)) if other != index]
        backs["out"], *backs[index] = call(
            functools.partial(last_backward_kernel, groups, index),
            [((rows, width), BF16)] * 2 + [((blocks, rows, LANES), F32)],
            [VMEM] * 11 + [ANY] + [VMEM] * (3 * len(others)),
            [pltpu.VMEM(shape, dtype) for shape, dtype in partial]
            + [pltpu.VMEM((width, rows), BF16), pltpu.VMEM((width, rows), F32)]
            + [pltpu.VMEM((rows, width), BF16), pltpu.SemaphoreType.DMA((2,))],
            in_hbm=2,
            **cost(size, rows, 4),
        )(*given, lanes, near_back, backs["out"], after, *[terms[i] for i in range(3) for terms in others])

    after = send
    for at, step in enumerate(reversed(steps)):
        if at:
            half = terms.shape[0] // 2
            send, terms = terms[half:], terms[:half]
        arrived = swap(send, step)
        if at == 0:
            backs["near"] = call(
                functools.partial(near_backward_kernel, heads),
                [((width, rows), F32), ((near_rows, 2 * width), BF16)],
                [VMEM] * 8 + [ANY],
                [pltpu.VMEM((near_rows, 2 * width), F32)],
                **cost(heads, near_rows, 4),
            )(near_came, far, qt, gt, near_p, ds, near_factor, delta, after)
        if at == 1:
            near_back = swap(backs["near"][1], 1)
        if at < len(groups):
            back(back_order[at], after)
            arrived = tie(arrived, backs, back_order[at])
        after = arrived
        terms = terms + arrived.astype(F32)

    dq, sums = backs[back_order[-1]]
    key_gradient, value_gradient = call(
        combine_kernel,
        [((rows, width), BF16)] * 2,
        [VMEM] * 3,
        moved=12 * rows * width,
    )(lanes, sums, terms)
    return backs["out"], dq, key_gradient, value_gradient


def solution(mesh):
    split = P(("grp", "seq", "sub"), "hd")
    return jax.shard_map(
        local,
        mesh=mesh,
        in_specs=(split, split, split, split, P(), P(), P("grp")),
        out_specs=(split, split, split, split),
        check_vma=False,
    )
```

```python
import functools
import math

import jax
import jax.numpy as jnp
from jax import lax
from jax.experimental import pallas as pl
from jax.experimental.pallas import tpu as pltpu
from jax.sharding import PartitionSpec as P

HEAD_WIDTH = 48
CENTER_DILATION = 8
WIDE_DILATION = 128
LANES = 128
STACK = 256
ONES = 16
OUT_AT = 2
DEAD = -1e30
SCALE = HEAD_WIDTH**-0.5
EXP2_SCALE = SCALE * math.log2(math.e)
F32 = jnp.float32
BF16 = jnp.bfloat16

VMEM = pl.BlockSpec(memory_space=pltpu.VMEM)
SMEM = pl.BlockSpec(memory_space=pltpu.SMEM)


def nn(a, b):
    return jnp.dot(a, b, preferred_element_type=F32)


def nt(a, b):
    return lax.dot_general(a, b, (((1,), (1,)), ((), ())), preferred_element_type=F32)


def head_rows(h):
    return slice(h * HEAD_WIDTH, (h + 1) * HEAD_WIDTH)


def window(h):
    low = h * HEAD_WIDTH // LANES * LANES
    high = -(-(h + 1) * HEAD_WIDTH // LANES) * LANES
    return low, high


def embed(rows, h):
    low, high = window(h)
    before, after = h * HEAD_WIDTH - low, high - (h + 1) * HEAD_WIDTH
    parts = [rows]
    if before:
        parts.insert(0, jnp.zeros((before, rows.shape[1]), rows.dtype))
    if after:
        parts.append(jnp.zeros((after, rows.shape[1]), rows.dtype))
    return jnp.concatenate(parts, axis=0) if len(parts) > 1 else rows


def head_groups(heads):
    edge = max(1, heads // 4)
    return [(0, edge), (edge, heads - edge), (heads - edge, heads)]


def lane_shifts(shift_ref, base, heads, width):
    lane = lax.broadcasted_iota(jnp.int32, (1, width), 1)
    row = jnp.zeros((1, width), jnp.int32)
    for h in range(heads):
        inside = (lane >= h * HEAD_WIDTH) & (lane < (h + 1) * HEAD_WIDTH)
        row = jnp.where(inside, shift_ref[base + h], row)
    return row


def head_base(heads):
    return lax.axis_index("hd") * heads


def select_kernel(
    heads, center_any, wide_any, q_any, k_any, v_any,
    far_ref, q_ref, k_ref, v_ref, table_ref, lanes_ref,
    center_ref, wide_ref, sems,
):
    rows, width = k_ref.shape
    pairs = (
        (center_any, center_ref), (wide_any, wide_ref),
        (k_any, k_ref), (v_any, v_ref), (q_any, q_ref),
    )
    copies = [pltpu.make_async_copy(a, b, sems.at[i]) for i, (a, b) in enumerate(pairs)]
    for copy in copies:
        copy.start()
    for copy in copies[:2]:
        copy.wait()
    base = head_base(heads)
    center = lane_shifts(center_ref, base, heads, width)
    wide = lane_shifts(wide_ref, base, heads, width)
    lanes_ref[0:1, :] = center
    lanes_ref[1:2, :] = wide
    for h in range(heads):
        table_ref[h : h + 1, :] = jnp.full((1, rows), center_ref[base + h], jnp.int32)
        table_ref[heads + h : heads + h + 1, :] = jnp.full((1, rows), wide_ref[base + h], jnp.int32)
    far_rows = rows // WIDE_DILATION
    row = lax.broadcasted_iota(jnp.int32, (far_rows, WIDE_DILATION, LANES), 1)
    for at, ref, copy in ((0, k_ref, copies[2]), (width, v_ref, copies[3])):
        copy.wait()
        for low in range(0, width, LANES):
            lanes = slice(low, low + LANES)
            packed = slice(at + low, at + low + LANES)
            spread = ref[:, lanes].astype(F32)
            chosen = jnp.where(row == wide[:, lanes], spread.reshape(row.shape), 0.0)
            far_ref[:, packed] = jnp.sum(chosen, axis=1).astype(BF16)
    copies[4].wait()


def forward_heads(
    group, heads, valid_ref, table_ref, k_ref, qt_ref, vt_ref, p_ref, ot_ref, max_ref, sum_ref
):
    first, last = group
    rows = k_ref.shape[0]
    device = lax.axis_index(("seq", "sub"))
    row = lax.broadcasted_iota(jnp.int32, (rows, LANES), 0)
    dead = jnp.where(device * rows + row < valid_ref[0], 0.0, DEAD)
    ones = jnp.ones((ONES, rows), BF16)

    def scores_of(h):
        low, high = window(h)
        is_near = (row & (CENTER_DILATION - 1)) == table_ref[h : h + 1, :LANES]
        is_far = (row & (WIDE_DILATION - 1)) == table_ref[heads + h : heads + h + 1, :LANES]
        once = jnp.where(is_near | is_far, 1.0 / EXP2_SCALE, 0.0)
        bias = dead + jnp.where(is_near & is_far, math.log2(3) / EXP2_SCALE, once)
        scores = nn(k_ref[:, low:high], embed(qt_ref[head_rows(h), :], h)) + widen(bias, rows)
        return scores, jnp.max(scores, axis=0, keepdims=True)

    following = scores_of(first)
    for h in range(first, last):
        scores, top = following
        if h + 1 < last:
            following = scores_of(h + 1)
        at = h - first
        weights = jnp.exp2((scores - top) * EXP2_SCALE).astype(BF16)
        p_ref[at] = weights
        summed = nn(jnp.concatenate([vt_ref[head_rows(h), :], ones], axis=0), weights)
        max_ref[at : at + 1, :] = top
        sum_ref[at : at + 1, :] = summed[HEAD_WIDTH : HEAD_WIDTH + 1]
        ot_ref[head_rows(at), :] = summed[:HEAD_WIDTH]


def select_near(center_ref, source_ref, near_ref, at0, spread_ref):
    rows, width = source_ref.shape
    near_rows = rows // CENTER_DILATION
    for low in range(0, width, LANES):
        lanes = slice(low, low + LANES)
        spread_ref[low // LANES] = source_ref[:, lanes].astype(F32)
    for low in range(0, width, LANES):
        lanes = slice(low, low + LANES)
        picked = jnp.zeros((near_rows, LANES), F32)
        for step in range(CENTER_DILATION):
            strided = pl.ds(step, near_rows, stride=CENTER_DILATION)
            picked = jnp.where(center_ref[0:1, lanes] == step, spread_ref[low // LANES, strided, :], picked)
        near_ref[:, at0 + low : at0 + low + LANES] = picked.astype(BF16)


def first_forward_kernel(
    group, heads, valid_ref, table_ref, k_ref, q_ref, v_ref, lanes_ref, after_ref,
    near_ref, qt_ref, vt_ref, *refs,
):
    *outs, spread_ref = refs
    select_near(lanes_ref, k_ref, near_ref, 0, spread_ref.at[0])
    select_near(lanes_ref, v_ref, near_ref, v_ref.shape[1], spread_ref.at[1])
    qt_ref[...] = q_ref[...].T
    vt_ref[...] = v_ref[...].T
    forward_heads(group, heads, valid_ref, table_ref, k_ref, qt_ref, vt_ref, *outs)


def forward_kernel(group, heads, valid_ref, table_ref, k_ref, qt_ref, vt_ref, after_ref, *outs):
    forward_heads(group, heads, valid_ref, table_ref, k_ref, qt_ref, vt_ref, *outs)


def stacks(heads, count):
    size = max(1, min(heads, STACK // count))
    found = []
    for first in range(0, heads, size):
        last = min(first + size, heads)
        found.append((first, last, window(first)[0], window(last - 1)[1]))
    return found


def head_lanes(h, low, high):
    lane = low + lax.broadcasted_iota(jnp.int32, (1, high - low), 1)
    return (lane >= h * HEAD_WIDTH) & (lane < (h + 1) * HEAD_WIDTH)


def stacked(rows, stack):
    first, last, low, high = stack
    return jnp.concatenate(
        [rows[:, low:high] * head_lanes(h, low, high).astype(F32).astype(BF16) for h in range(first, last)],
        axis=0,
    )


def unstack(ref, at0, stack, count, value, by, started):
    first, last, low, high = stack
    total = None
    for at, h in enumerate(range(first, last)):
        part = jnp.where(head_lanes(h, low, high), value[at * count : (at + 1) * count], 0.0)
        total = part if total is None else total + part
    total = total * by
    for at in range(low, high, LANES):
        part = total[:, at - low : at - low + LANES]
        if (at0, at) in started:
            ref[:, at0 + at : at0 + at + LANES] += part
        else:
            started.add((at0, at))
            ref[:, at0 + at : at0 + at + LANES] = part


def widen(value, rows):
    return jnp.concatenate([value] * (rows // LANES), axis=1)


def near_forward_kernel(heads, groups, valid_ref, table_ref, near_ref, qt_ref, k_ref, g_ref, *refs):
    parts = len(groups)
    o1_refs, max_refs, sum_refs = (refs[i * parts : (i + 1) * parts] for i in range(3))
    after_ref, gt_ref, kt_ref, p_ref, o_ref, old_ref, top_ref, sum_ref = refs[3 * parts :]
    gt_ref[...] = g_ref[...].T
    kt_ref[...] = k_ref[...].T
    width, rows = qt_ref.shape
    count = near_ref.shape[0]
    device = lax.axis_index(("seq", "sub"))
    row = lax.broadcasted_iota(jnp.int32, (count, LANES), 0)
    room = valid_ref[0] - ((device ^ 1) * rows + row * CENTER_DILATION)
    where = {}
    for part, (first, last) in enumerate(groups):
        for h in range(first, last):
            where[h] = part, h - first
    for stack in stacks(heads, count):
        first, last, low, high = stack
        scores = nn(stacked(near_ref[:, :width], stack), qt_ref[low:high, :])
        lifts, keeps = [], []
        for at, h in enumerate(range(first, last)):
            part, index = where[h]
            dead = jnp.where(table_ref[h : h + 1, :LANES] < room, 0.0, DEAD)
            here = scores[at * count : (at + 1) * count] + widen(dead, rows)
            old = max_refs[part][index : index + 1, :]
            top = jnp.maximum(jnp.max(here, axis=0, keepdims=True), old)
            lifted = jnp.exp2((here - top) * EXP2_SCALE)
            keep = jnp.exp2((old - top) * EXP2_SCALE)
            old_ref[h : h + 1, :] = old
            top_ref[h : h + 1, :] = top
            sum_ref[h : h + 1, :] = sum_refs[part][index : index + 1, :] * keep + jnp.sum(
                lifted, axis=0, keepdims=True
            )
            keeps.append(keep)
            lifts.append(lifted.astype(BF16))
        weights = jnp.concatenate(lifts, axis=0)
        p_ref[first * count : last * count, :] = weights
        added = nn(stacked(near_ref[:, width:], stack).T, weights)
        for keep, h in zip(keeps, range(first, last)):
            part, index = where[h]
            inside = added[h * HEAD_WIDTH - low : (h + 1) * HEAD_WIDTH - low]
            o_ref[head_rows(h), :] = o1_refs[part][head_rows(index), :] * keep + inside


def wide_kernel(
    heads, far_own, valid_ref, table_ref, far_ref, qt_ref, gt_ref, o_ref, old_ref, near_top_ref, near_sum_ref,
    ot_ref, local_ref, near_ref, delta_ref, ds_ref, keep_ref, send_ref, sum_ref,
):
    width, rows = qt_ref.shape
    count = far_ref.shape[0]
    half = count // 2
    device = lax.axis_index(("seq", "sub"))
    row = lax.broadcasted_iota(jnp.int32, (count, LANES), 0)
    slot = lax.shift_right_arithmetic(row, far_own.bit_length() - 1)
    place = (device ^ slot) * rows + (row & (far_own - 1)) * WIDE_DILATION
    room = jnp.where(slot == 0, -1, valid_ref[0] - place)
    started = set()
    for stack in stacks(heads, count):
        first, last, low, high = stack
        value_rows = stacked(far_ref[:, width:], stack)
        scores = nn(stacked(far_ref[:, :width], stack), qt_ref[low:high, :])
        grad_prob = nn(value_rows, gt_ref[low:high, :])
        probs, factors = [], []
        for at, h in enumerate(range(first, last)):
            one = slice(h, h + 1)
            dead = jnp.where(table_ref[heads + h : heads + h + 1, :LANES] < room, 0.0, DEAD)
            here = scores[at * count : (at + 1) * count] + widen(dead, rows)
            near_top = near_top_ref[one, :]
            top = jnp.maximum(jnp.max(here, axis=0, keepdims=True), near_top)
            lifted = jnp.exp2((here - top) * EXP2_SCALE)
            keep = jnp.exp2((near_top - top) * EXP2_SCALE)
            inverse = 1.0 / (near_sum_ref[one, :] * keep + jnp.sum(lifted, axis=0, keepdims=True))
            probs.append(lifted * inverse)
            factors.append(keep * inverse)
            near_ref[one, :] = keep * inverse
            local_ref[one, :] = jnp.exp2((old_ref[one, :] - top) * EXP2_SCALE) * inverse
        weights = jnp.concatenate([prob.astype(BF16) for prob in probs], axis=0)
        added = nn(value_rows.T, weights)
        unstack(sum_ref, width, stack, count, nt(weights, gt_ref[low:high, :]), 1.0, started)
        dscores = []
        for at, h in enumerate(range(first, last)):
            inside = added[h * HEAD_WIDTH - low : (h + 1) * HEAD_WIDTH - low]
            context = o_ref[head_rows(h), :] * factors[at] + inside
            ot_ref[head_rows(h), :] = context.astype(BF16)
            delta = jnp.sum(gt_ref[head_rows(h), :].astype(F32) * context, axis=0, keepdims=True)
            delta_ref[h : h + 1, :] = delta
            here = grad_prob[at * count : (at + 1) * count]
            dscores.append((probs[at] * (here - delta)).astype(BF16))
        dscore = jnp.concatenate(dscores, axis=0)
        ds_ref[first * count : last * count, :] = dscore
        unstack(sum_ref, 0, stack, count, nt(dscore, qt_ref[low:high, :]), SCALE, started)
    keep_ref[...] = sum_ref[:half, :]
    send_ref[...] = sum_ref[half:, :].astype(send_ref.dtype)


def near_backward_kernel(
    heads, near_ref, far_ref, qt_ref, gt_ref, p_ref, ds_ref, factor_ref, delta_ref, after_ref,
    dq_ref, send_ref, sum_ref,
):
    width, rows = qt_ref.shape
    count = near_ref.shape[0]
    started, begun = set(), set()

    def add_dq(stack, product):
        first, last, low, _ = stack
        for h in range(first, last):
            inside = product[h * HEAD_WIDTH - low : (h + 1) * HEAD_WIDTH - low]
            if h in begun:
                dq_ref[head_rows(h), :] += inside
            else:
                begun.add(h)
                dq_ref[head_rows(h), :] = inside

    for stack in stacks(heads, count):
        first, last, low, high = stack
        grad_prob = nn(stacked(near_ref[:, width:], stack), gt_ref[low:high, :])
        weights, dscores = [], []
        for at, h in enumerate(range(first, last)):
            prob = p_ref[h * count : (h + 1) * count, :].astype(F32) * factor_ref[h : h + 1, :]
            here = grad_prob[at * count : (at + 1) * count]
            weights.append(prob.astype(BF16))
            dscores.append((prob * (here - delta_ref[h : h + 1, :])).astype(BF16))
        dscore = jnp.concatenate(dscores, axis=0)
        add_dq(stack, nn(stacked(near_ref[:, :width], stack).T, dscore))
        unstack(sum_ref, 0, stack, count, nt(dscore, qt_ref[low:high, :]), SCALE, started)
        weight = jnp.concatenate(weights, axis=0)
        unstack(sum_ref, width, stack, count, nt(weight, gt_ref[low:high, :]), 1.0, started)
    send_ref[...] = sum_ref[...].astype(send_ref.dtype)
    count = far_ref.shape[0]
    for stack in stacks(heads, count):
        first, last, _, _ = stack
        dscore = ds_ref[first * count : last * count, :]
        add_dq(stack, nn(stacked(far_ref[:, :width], stack).T, dscore))


def backward_heads(
    group, p_ref, qt_ref, gt_ref, kt_ref, v_ref, dq2_ref, factor_ref, delta_ref, dqt_ref, dk_ref, dv_ref
):
    first, last = group
    rows = v_ref.shape[0]
    parts = [slice(at, at + rows // 2) for at in (0, rows // 2)]
    work = [(h, part) for h in range(first, last) for part in parts]

    def product(h, part):
        low, high = window(h)
        return nn(v_ref[part, low:high], embed(gt_ref[head_rows(h), :], h))

    following = product(*work[0])
    for index, (h, part) in enumerate(work):
        grad_prob = following
        if index + 1 < len(work):
            following = product(*work[index + 1])
        at, head = h - first, head_rows(h)
        here = head_rows(at)
        prob = p_ref[at, part, :].astype(F32) * factor_ref[h : h + 1, :]
        dv_ref[here, part] = nt(gt_ref[head, :], prob.astype(BF16))
        dscore = (prob * (grad_prob - delta_ref[h : h + 1, :])).astype(BF16)
        dk_ref[here, part] = nt(qt_ref[head, :], dscore)
        term = nn(kt_ref[head, part], dscore)
        dqt = term + (dq2_ref[head, :] if part is parts[0] else dqt)
        if part is parts[1]:
            dqt_ref[here, :] = (dqt * SCALE).astype(BF16)


def backward_kernel(group, *refs):
    backward_heads(group, *refs[:8], *refs[9:])


def turning_backward_kernel(group, *refs):
    ot_ref, out_ref = refs[9:11]
    backward_heads(group, *refs[:8], *refs[11:])
    out_ref[...] = ot_ref[...].T


def last_backward_kernel(groups, index, *refs):
    others = len(groups) - 1
    lanes_ref, back_ref, out_ref, after_ref = refs[8:12]
    terms = refs[12 : 12 + 3 * others]
    out_any, dq_any, sum_ref, dqt_ref, dk_ref, dv_ref, turned_ref, wide_ref, dq_ref, sems = refs[12 + 3 * others :]
    copies = [
        pltpu.make_async_copy(out_ref, out_any, sems.at[0]),
        pltpu.make_async_copy(dq_ref, dq_any, sems.at[1]),
    ]
    copies[0].start()
    backward_heads(groups[index], *refs[:8], dqt_ref, dk_ref, dv_ref)

    def all_groups(at, mine):
        found = list(terms[at * others : (at + 1) * others])
        found.insert(index, mine)
        return found

    rows, width = dq_ref.shape
    near_rows = rows // CENTER_DILATION
    for (first, last), ref in zip(groups, all_groups(0, dqt_ref)):
        turned_ref[first * HEAD_WIDTH : last * HEAD_WIDTH, :] = ref[...]
    dq_ref[...] = turned_ref[...].T
    copies[1].start()
    for at, parts, by in ((0, all_groups(1, dk_ref), SCALE), (width, all_groups(2, dv_ref), 1.0)):
        for (first, last), ref in zip(groups, parts):
            wide_ref[first * HEAD_WIDTH : last * HEAD_WIDTH, :] = ref[...] * by
        for low in range(0, width, LANES):
            block = (at + low) // LANES
            sum_ref[block] = wide_ref[low : low + LANES, :].T
            near = back_ref[:, at + low : at + low + LANES].astype(F32)
            center = lanes_ref[0:1, low : low + LANES]
            for step in range(CENTER_DILATION):
                strided = pl.ds(step, near_rows, stride=CENTER_DILATION)
                sum_ref[block, strided, :] += jnp.where(center == step, near, 0.0)
    for copy in copies:
        copy.wait()


def combine_kernel(lanes_ref, sum_ref, far_ref, outk_ref, outv_ref):
    rows, width = outk_ref.shape
    far_rows = far_ref.shape[0]
    row = lax.broadcasted_iota(jnp.int32, (WIDE_DILATION, LANES), 0)
    for at, out in ((0, outk_ref), (width, outv_ref)):
        for low in range(0, width, LANES):
            block = (at + low) // LANES
            mask = row == lanes_ref[1:2, low : low + LANES]
            for index in range(far_rows):
                part = slice(index * WIDE_DILATION, (index + 1) * WIDE_DILATION)
                far = far_ref[index : index + 1, at + low : at + low + LANES]
                value = sum_ref[block, part, :] + jnp.where(mask, far, 0.0)
                out[part, low : low + LANES] = value.astype(BF16)


ANY = pl.BlockSpec(memory_space=pl.ANY)
HBM = pl.BlockSpec(memory_space=pltpu.HBM)


def call(body, outs, ins, scratch=(), *, in_hbm=0, flops=0, moved=0):
    return pl.pallas_call(
        body,
        out_shape=[jax.ShapeDtypeStruct(s, d) for s, d in outs],
        in_specs=ins,
        out_specs=[HBM] * in_hbm + [VMEM] * (len(outs) - in_hbm),
        scratch_shapes=list(scratch),
        compiler_params=pltpu.CompilerParams(vmem_limit_bytes=24 * 2**20),
        cost_estimate=pl.CostEstimate(flops=flops, bytes_accessed=moved, transcendentals=0),
    )


def local(queries, keys, values, grad_out, center_shift, wide_shift, valid_count):
    rows, width = queries.shape
    heads = width // HEAD_WIDTH
    groups = head_groups(heads)
    near_rows, far_own = rows // CENTER_DILATION, rows // WIDE_DILATION
    axes = ("seq", "sub")
    devices = lax.axis_size(axes)
    far_rows = far_own * devices
    blocks = 2 * width // LANES
    steps = [2**bit for bit in range(devices.bit_length() - 1)]

    def swap(value, apart):
        return lax.ppermute(value, axes, [(at, at ^ apart) for at in range(devices)])

    far, q, k, v, table, lanes = call(
        functools.partial(select_kernel, heads),
        [((far_own, 2 * width), BF16)]
        + [((rows, width), BF16)] * 3
        + [((2 * heads, rows), jnp.int32), ((8, width), jnp.int32)],
        [HBM] * 5,
        [
            pltpu.SMEM(center_shift.shape, jnp.int32),
            pltpu.SMEM(wide_shift.shape, jnp.int32),
            pltpu.SemaphoreType.DMA((5,)),
        ],
        moved=16 * rows * width,
    )(
        *(
            pltpu.with_memory_space_constraint(value, pltpu.HBM)
            for value in (center_shift, wide_shift, queries, keys, values)
        )
    )

    valid, far = lax.optimization_barrier((valid_count, far))

    def cost(heads_done, keys_done, products):
        done = heads_done * keys_done * rows
        return dict(flops=2 * HEAD_WIDTH * done * products * 5, moved=2 * done)

    turned = {}
    fronts = {}

    def front(index, after):
        first, last = groups[index]
        size, tall = last - first, (last - first) * HEAD_WIDTH
        outs = [((size, rows, rows), BF16), ((tall, rows), F32), ((size, rows), F32), ((size, rows), F32)]
        if not turned:
            *flipped, p, o, top, total = call(
                functools.partial(first_forward_kernel, groups[index], heads),
                [((near_rows, 2 * width), BF16)] + [((width, rows), BF16)] * 2 + outs,
                [SMEM] + [VMEM] * 5 + [ANY],
                [pltpu.VMEM((2, blocks // 2, rows, LANES), F32)],
                **cost(size, rows, 2),
            )(valid, table, k, q, v, lanes, after)
            turned.update(zip(("near", "qt", "vt"), flipped))
        else:
            p, o, top, total = call(
                functools.partial(forward_kernel, groups[index], heads),
                outs,
                [SMEM] + [VMEM] * 4 + [ANY],
                **cost(size, rows, 2),
            )(valid, table, k, turned["qt"], turned["vt"], after)
        fronts[index] = [p, o, top, total]

    def tie(arrived, holder, key):
        arrived, held = lax.optimization_barrier((arrived, holder[key][-1]))
        holder[key] = [*holder[key][:-1], held]
        return arrived

    last = len(groups) - 1
    front_order, back_order = [last, *range(last)], [*range(last, -1, -1)]
    after = far
    for at, step in enumerate(steps):
        if at == 1:
            near_out, far = lax.optimization_barrier((turned["near"], far))
        arrived = swap(far, step)
        if at == 1:
            near_came = swap(near_out, 1)
        if at < len(groups):
            front(front_order[at], after)
        if at == len(groups) - 1:
            p, o, top, total = zip(*(fronts[index] for index in range(len(groups))))
            fronts["near"] = call(
                functools.partial(near_forward_kernel, heads, groups),
                [((width, rows), BF16)] * 2
                + [((heads * near_rows, rows), BF16), ((width, rows), F32)]
                + [((heads, rows), F32)] * 3,
                [SMEM] + [VMEM] * (5 + 3 * len(groups)) + [ANY],
                **cost(heads, near_rows, 2),
            )(valid, table, near_came, turned["qt"], k, grad_out, *o, *top, *total, after)
            arrived = tie(arrived, fronts, "near")
        elif at < len(groups):
            arrived = tie(arrived, fronts, front_order[at])
        after = arrived
        far = jnp.concatenate([far, arrived], axis=0)
    gt, kt, near_p, o, old, near_top, near_sum = fronts["near"]
    qt = turned["qt"]

    ot, local_factor, near_factor, delta, ds, terms, send = call(
        functools.partial(wide_kernel, heads, far_own),
        [((width, rows), BF16)]
        + [((heads, rows), F32)] * 3
        + [((heads * far_rows, rows), BF16)]
        + [((far_rows // 2, 2 * width), F32)] * 2,
        [SMEM] + [VMEM] * 8,
        [pltpu.VMEM((far_rows, 2 * width), F32)],
        **cost(heads, far_rows, 5),
    )(valid, table, far, qt, gt, o, old, near_top, near_sum)

    backs = {}

    def back(index, after):
        first, end = groups[index]
        size, tall = end - first, (end - first) * HEAD_WIDTH
        partial = [((tall, rows), BF16), ((tall, rows), F32), ((tall, rows), F32)]
        given = (p[index], qt, gt, kt, v, backs["near"][0], local_factor, delta)
        if len(backs) == OUT_AT:
            backs["out"], *backs[index] = call(
                functools.partial(turning_backward_kernel, groups[index]),
                [((rows, width), BF16), *partial],
                [VMEM] * 8 + [ANY, VMEM],
                **cost(size, rows, 4),
            )(*given, after, ot)
            return
        if len(backs) < len(groups):
            backs[index] = call(
                functools.partial(backward_kernel, groups[index]),
                partial,
                [VMEM] * 8 + [ANY],
                **cost(size, rows, 4),
            )(*given, after)
            return
        others = [backs[other] for other in range(len(groups)) if other != index]
        backs["out"], *backs[index] = call(
            functools.partial(last_backward_kernel, groups, index),
            [((rows, width), BF16)] * 2 + [((blocks, rows, LANES), F32)],
            [VMEM] * 11 + [ANY] + [VMEM] * (3 * len(others)),
            [pltpu.VMEM(shape, dtype) for shape, dtype in partial]
            + [pltpu.VMEM((width, rows), BF16), pltpu.VMEM((width, rows), F32)]
            + [pltpu.VMEM((rows, width), BF16), pltpu.SemaphoreType.DMA((2,))],
            in_hbm=2,
            **cost(size, rows, 4),
        )(*given, lanes, near_back, backs["out"], after, *[terms[i] for i in range(3) for terms in others])

    after = send
    for at, step in enumerate(reversed(steps)):
        if at:
            half = terms.shape[0] // 2
            send, terms = terms[half:], terms[:half]
        arrived = swap(send, step)
        if at == 0:
            backs["near"] = call(
                functools.partial(near_backward_kernel, heads),
                [((width, rows), F32), ((near_rows, 2 * width), BF16)],
                [VMEM] * 8 + [ANY],
                [pltpu.VMEM((near_rows, 2 * width), F32)],
                **cost(heads, near_rows, 4),
            )(near_came, far, qt, gt, near_p, ds, near_factor, delta, after)
        if at == 1:
            near_back = swap(backs["near"][1], 1)
        if at < len(groups):
            back(back_order[at], after)
            arrived = tie(arrived, backs, back_order[at])
        after = arrived
        terms = terms + arrived.astype(F32)

    dq, sums = backs[back_order[-1]]
    key_gradient, value_gradient = call(
        combine_kernel,
        [((rows, width), BF16)] * 2,
        [VMEM] * 3,
        moved=12 * rows * width,
    )(lanes, sums, terms)
    return backs["out"], dq, key_gradient, value_gradient


def solution(mesh):
    split = P(("grp", "seq", "sub"), "hd")
    return jax.shard_map(
        local,
        mesh=mesh,
        in_specs=(split, split, split, split, P(), P(), P("grp")),
        out_specs=(split, split, split, split),
        check_vma=False,
    )
```

```python
import functools
import math

import jax
import jax.numpy as jnp
from jax import lax
from jax.experimental import pallas as pl
from jax.experimental.pallas import tpu as pltpu
from jax.sharding import PartitionSpec as P

HEAD_WIDTH = 48
CENTER_DILATION = 8
WIDE_DILATION = 128
LANES = 128
STACK = 256
ONES = 16
OUT_AT = 2
DEAD = -1e30
SCALE = HEAD_WIDTH**-0.5
EXP2_SCALE = SCALE * math.log2(math.e)
F32 = jnp.float32
BF16 = jnp.bfloat16

VMEM = pl.BlockSpec(memory_space=pltpu.VMEM)
SMEM = pl.BlockSpec(memory_space=pltpu.SMEM)


def nn(a, b):
    return jnp.dot(a, b, preferred_element_type=F32)


def nt(a, b):
    return lax.dot_general(a, b, (((1,), (1,)), ((), ())), preferred_element_type=F32)


def head_rows(h):
    return slice(h * HEAD_WIDTH, (h + 1) * HEAD_WIDTH)


def window(h):
    low = h * HEAD_WIDTH // LANES * LANES
    high = -(-(h + 1) * HEAD_WIDTH // LANES) * LANES
    return low, high


def embed(rows, h):
    low, high = window(h)
    before, after = h * HEAD_WIDTH - low, high - (h + 1) * HEAD_WIDTH
    parts = [rows]
    if before:
        parts.insert(0, jnp.zeros((before, rows.shape[1]), rows.dtype))
    if after:
        parts.append(jnp.zeros((after, rows.shape[1]), rows.dtype))
    return jnp.concatenate(parts, axis=0) if len(parts) > 1 else rows


def head_groups(heads):
    edge = max(1, heads // 4)
    return [(0, edge), (edge, heads - edge), (heads - edge, heads)]


def lane_shifts(shift_ref, base, heads, width):
    lane = lax.broadcasted_iota(jnp.int32, (1, width), 1)
    row = jnp.zeros((1, width), jnp.int32)
    for h in range(heads):
        inside = (lane >= h * HEAD_WIDTH) & (lane < (h + 1) * HEAD_WIDTH)
        row = jnp.where(inside, shift_ref[base + h], row)
    return row


def head_base(heads):
    return lax.axis_index("hd") * heads


def select_kernel(
    heads, center_any, wide_any, q_any, k_any, v_any,
    far_ref, q_ref, k_ref, v_ref, table_ref, lanes_ref,
    center_ref, wide_ref, sems,
):
    rows, width = k_ref.shape
    pairs = (
        (center_any, center_ref), (wide_any, wide_ref),
        (k_any, k_ref), (v_any, v_ref), (q_any, q_ref),
    )
    copies = [pltpu.make_async_copy(a, b, sems.at[i]) for i, (a, b) in enumerate(pairs)]
    for copy in copies:
        copy.start()
    for copy in copies[:2]:
        copy.wait()
    base = head_base(heads)
    center = lane_shifts(center_ref, base, heads, width)
    wide = lane_shifts(wide_ref, base, heads, width)
    lanes_ref[0:1, :] = center
    lanes_ref[1:2, :] = wide
    for h in range(heads):
        table_ref[h : h + 1, :] = jnp.full((1, rows), center_ref[base + h], jnp.int32)
        table_ref[heads + h : heads + h + 1, :] = jnp.full((1, rows), wide_ref[base + h], jnp.int32)
    far_rows = rows // WIDE_DILATION
    row = lax.broadcasted_iota(jnp.int32, (far_rows, WIDE_DILATION, LANES), 1)
    for at, ref, copy in ((0, k_ref, copies[2]), (width, v_ref, copies[3])):
        copy.wait()
        for low in range(0, width, LANES):
            lanes = slice(low, low + LANES)
            packed = slice(at + low, at + low + LANES)
            spread = ref[:, lanes].astype(F32)
            chosen = jnp.where(row == wide[:, lanes], spread.reshape(row.shape), 0.0)
            far_ref[:, packed] = jnp.sum(chosen, axis=1).astype(BF16)
    copies[4].wait()


def forward_heads(
    group, heads, valid_ref, table_ref, k_ref, qt_ref, vt_ref, p_ref, ot_ref, max_ref, sum_ref
):
    first, last = group
    rows = k_ref.shape[0]
    device = lax.axis_index(("seq", "sub"))
    row = lax.broadcasted_iota(jnp.int32, (rows, LANES), 0)
    dead = jnp.where(device * rows + row < valid_ref[0], 0.0, DEAD)
    ones = jnp.ones((ONES, rows), BF16)

    def scores_of(h):
        low, high = window(h)
        is_near = (row & (CENTER_DILATION - 1)) == table_ref[h : h + 1, :LANES]
        is_far = (row & (WIDE_DILATION - 1)) == table_ref[heads + h : heads + h + 1, :LANES]
        once = jnp.where(is_near | is_far, 1.0 / EXP2_SCALE, 0.0)
        bias = dead + jnp.where(is_near & is_far, math.log2(3) / EXP2_SCALE, once)
        scores = nn(k_ref[:, low:high], embed(qt_ref[head_rows(h), :], h)) + widen(bias, rows)
        return scores, jnp.max(scores, axis=0, keepdims=True)

    following = scores_of(first)
    for h in range(first, last):
        scores, top = following
        if h + 1 < last:
            following = scores_of(h + 1)
        at = h - first
        weights = jnp.exp2((scores - top) * EXP2_SCALE).astype(BF16)
        p_ref[at] = weights
        summed = nn(jnp.concatenate([vt_ref[head_rows(h), :], ones], axis=0), weights)
        max_ref[at : at + 1, :] = top
        sum_ref[at : at + 1, :] = summed[HEAD_WIDTH : HEAD_WIDTH + 1]
        ot_ref[head_rows(at), :] = summed[:HEAD_WIDTH]


def select_near(center_ref, source_ref, near_ref, at0, spread_ref):
    rows, width = source_ref.shape
    near_rows = rows // CENTER_DILATION
    for low in range(0, width, LANES):
        lanes = slice(low, low + LANES)
        spread_ref[low // LANES] = source_ref[:, lanes].astype(F32)
    for low in range(0, width, LANES):
        lanes = slice(low, low + LANES)
        picked = jnp.zeros((near_rows, LANES), F32)
        for step in range(CENTER_DILATION):
            strided = pl.ds(step, near_rows, stride=CENTER_DILATION)
            picked = jnp.where(center_ref[0:1, lanes] == step, spread_ref[low // LANES, strided, :], picked)
        near_ref[:, at0 + low : at0 + low + LANES] = picked.astype(BF16)


def first_forward_kernel(
    group, heads, valid_ref, table_ref, k_ref, q_ref, v_ref, lanes_ref, after_ref,
    near_ref, qt_ref, vt_ref, *refs,
):
    *outs, spread_ref = refs
    select_near(lanes_ref, k_ref, near_ref, 0, spread_ref.at[0])
    select_near(lanes_ref, v_ref, near_ref, v_ref.shape[1], spread_ref.at[1])
    qt_ref[...] = q_ref[...].T
    vt_ref[...] = v_ref[...].T
    forward_heads(group, heads, valid_ref, table_ref, k_ref, qt_ref, vt_ref, *outs)


def forward_kernel(group, heads, valid_ref, table_ref, k_ref, qt_ref, vt_ref, after_ref, *outs):
    forward_heads(group, heads, valid_ref, table_ref, k_ref, qt_ref, vt_ref, *outs)


def stacks(heads, count):
    size = max(1, min(heads, STACK // count))
    found = []
    for first in range(0, heads, size):
        last = min(first + size, heads)
        found.append((first, last, window(first)[0], window(last - 1)[1]))
    return found


def head_lanes(h, low, high):
    lane = low + lax.broadcasted_iota(jnp.int32, (1, high - low), 1)
    return (lane >= h * HEAD_WIDTH) & (lane < (h + 1) * HEAD_WIDTH)


def stacked(rows, stack):
    first, last, low, high = stack
    return jnp.concatenate(
        [rows[:, low:high] * head_lanes(h, low, high).astype(F32).astype(BF16) for h in range(first, last)],
        axis=0,
    )


def unstack(ref, at0, stack, count, value, by, started):
    first, last, low, high = stack
    total = None
    for at, h in enumerate(range(first, last)):
        part = jnp.where(head_lanes(h, low, high), value[at * count : (at + 1) * count], 0.0)
        total = part if total is None else total + part
    total = total * by
    for at in range(low, high, LANES):
        part = total[:, at - low : at - low + LANES]
        if (at0, at) in started:
            ref[:, at0 + at : at0 + at + LANES] += part
        else:
            started.add((at0, at))
            ref[:, at0 + at : at0 + at + LANES] = part


def widen(value, rows):
    return jnp.concatenate([value] * (rows // LANES), axis=1)


def near_forward_kernel(heads, groups, valid_ref, table_ref, near_ref, qt_ref, k_ref, g_ref, *refs):
    parts = len(groups)
    o1_refs, max_refs, sum_refs = (refs[i * parts : (i + 1) * parts] for i in range(3))
    after_ref, gt_ref, kt_ref, p_ref, o_ref, old_ref, top_ref, sum_ref = refs[3 * parts :]
    gt_ref[...] = g_ref[...].T
    kt_ref[...] = k_ref[...].T
    width, rows = qt_ref.shape
    count = near_ref.shape[0]
    device = lax.axis_index(("seq", "sub"))
    row = lax.broadcasted_iota(jnp.int32, (count, LANES), 0)
    room = valid_ref[0] - ((device ^ 1) * rows + row * CENTER_DILATION)
    where = {}
    for part, (first, last) in enumerate(groups):
        for h in range(first, last):
            where[h] = part, h - first
    for stack in stacks(heads, count):
        first, last, low, high = stack
        scores = nn(stacked(near_ref[:, :width], stack), qt_ref[low:high, :])
        lifts, keeps = [], []
        for at, h in enumerate(range(first, last)):
            part, index = where[h]
            dead = jnp.where(table_ref[h : h + 1, :LANES] < room, 0.0, DEAD)
            here = scores[at * count : (at + 1) * count] + widen(dead, rows)
            old = max_refs[part][index : index + 1, :]
            top = jnp.maximum(jnp.max(here, axis=0, keepdims=True), old)
            lifted = jnp.exp2((here - top) * EXP2_SCALE)
            keep = jnp.exp2((old - top) * EXP2_SCALE)
            old_ref[h : h + 1, :] = old
            top_ref[h : h + 1, :] = top
            sum_ref[h : h + 1, :] = sum_refs[part][index : index + 1, :] * keep + jnp.sum(
                lifted, axis=0, keepdims=True
            )
            keeps.append(keep)
            lifts.append(lifted.astype(BF16))
        weights = jnp.concatenate(lifts, axis=0)
        p_ref[first * count : last * count, :] = weights
        added = nn(stacked(near_ref[:, width:], stack).T, weights)
        for keep, h in zip(keeps, range(first, last)):
            part, index = where[h]
            inside = added[h * HEAD_WIDTH - low : (h + 1) * HEAD_WIDTH - low]
            o_ref[head_rows(h), :] = o1_refs[part][head_rows(index), :] * keep + inside


def wide_kernel(
    heads, far_own, valid_ref, table_ref, far_ref, qt_ref, gt_ref, o_ref, old_ref, near_top_ref, near_sum_ref,
    ot_ref, local_ref, near_ref, delta_ref, ds_ref, keep_ref, send_ref, sum_ref,
):
    width, rows = qt_ref.shape
    count = far_ref.shape[0]
    half = count // 2
    device = lax.axis_index(("seq", "sub"))
    row = lax.broadcasted_iota(jnp.int32, (count, LANES), 0)
    slot = lax.shift_right_arithmetic(row, far_own.bit_length() - 1)
    place = (device ^ slot) * rows + (row & (far_own - 1)) * WIDE_DILATION
    room = jnp.where(slot == 0, -1, valid_ref[0] - place)
    started = set()
    for stack in stacks(heads, count):
        first, last, low, high = stack
        value_rows = stacked(far_ref[:, width:], stack)
        scores = nn(stacked(far_ref[:, :width], stack), qt_ref[low:high, :])
        grad_prob = nn(value_rows, gt_ref[low:high, :])
        probs, factors = [], []
        for at, h in enumerate(range(first, last)):
            one = slice(h, h + 1)
            dead = jnp.where(table_ref[heads + h : heads + h + 1, :LANES] < room, 0.0, DEAD)
            here = scores[at * count : (at + 1) * count] + widen(dead, rows)
            near_top = near_top_ref[one, :]
            top = jnp.maximum(jnp.max(here, axis=0, keepdims=True), near_top)
            lifted = jnp.exp2((here - top) * EXP2_SCALE)
            keep = jnp.exp2((near_top - top) * EXP2_SCALE)
            inverse = 1.0 / (near_sum_ref[one, :] * keep + jnp.sum(lifted, axis=0, keepdims=True))
            probs.append(lifted * inverse)
            factors.append(keep * inverse)
            near_ref[one, :] = keep * inverse
            local_ref[one, :] = jnp.exp2((old_ref[one, :] - top) * EXP2_SCALE) * inverse
        weights = jnp.concatenate([prob.astype(BF16) for prob in probs], axis=0)
        added = nn(value_rows.T, weights)
        unstack(sum_ref, width, stack, count, nt(weights, gt_ref[low:high, :]), 1.0, started)
        dscores = []
        for at, h in enumerate(range(first, last)):
            inside = added[h * HEAD_WIDTH - low : (h + 1) * HEAD_WIDTH - low]
            context = o_ref[head_rows(h), :] * factors[at] + inside
            ot_ref[head_rows(h), :] = context.astype(BF16)
            delta = jnp.sum(gt_ref[head_rows(h), :].astype(F32) * context, axis=0, keepdims=True)
            delta_ref[h : h + 1, :] = delta
            here = grad_prob[at * count : (at + 1) * count]
            dscores.append((probs[at] * (here - delta)).astype(BF16))
        dscore = jnp.concatenate(dscores, axis=0)
        ds_ref[first * count : last * count, :] = dscore
        unstack(sum_ref, 0, stack, count, nt(dscore, qt_ref[low:high, :]), SCALE, started)
    keep_ref[...] = sum_ref[:half, :]
    send_ref[...] = sum_ref[half:, :].astype(send_ref.dtype)


def near_backward_kernel(
    heads, near_ref, far_ref, qt_ref, gt_ref, p_ref, ds_ref, factor_ref, delta_ref, after_ref,
    dq_ref, send_ref, sum_ref,
):
    width, rows = qt_ref.shape
    count = near_ref.shape[0]
    started, begun = set(), set()

    def add_dq(stack, product):
        first, last, low, _ = stack
        for h in range(first, last):
            inside = product[h * HEAD_WIDTH - low : (h + 1) * HEAD_WIDTH - low]
            if h in begun:
                dq_ref[head_rows(h), :] += inside
            else:
                begun.add(h)
                dq_ref[head_rows(h), :] = inside

    for stack in stacks(heads, count):
        first, last, low, high = stack
        grad_prob = nn(stacked(near_ref[:, width:], stack), gt_ref[low:high, :])
        probs = [
            p_ref[h * count : (h + 1) * count, :].astype(F32) * factor_ref[h : h + 1, :]
            for h in range(first, last)
        ]
        weight = jnp.concatenate([prob.astype(BF16) for prob in probs], axis=0)
        unstack(sum_ref, width, stack, count, nt(weight, gt_ref[low:high, :]), 1.0, started)
        dscores = []
        for at, h in enumerate(range(first, last)):
            here = grad_prob[at * count : (at + 1) * count]
            dscores.append((probs[at] * (here - delta_ref[h : h + 1, :])).astype(BF16))
        dscore = jnp.concatenate(dscores, axis=0)
        unstack(sum_ref, 0, stack, count, nt(dscore, qt_ref[low:high, :]), SCALE, started)
        add_dq(stack, nn(stacked(near_ref[:, :width], stack).T, dscore))
    send_ref[...] = sum_ref[...].astype(send_ref.dtype)
    count = far_ref.shape[0]
    for stack in stacks(heads, count):
        first, last, _, _ = stack
        dscore = ds_ref[first * count : last * count, :]
        add_dq(stack, nn(stacked(far_ref[:, :width], stack).T, dscore))


def backward_heads(
    group, p_ref, qt_ref, gt_ref, kt_ref, v_ref, dq2_ref, factor_ref, delta_ref, dqt_ref, dk_ref, dv_ref
):
    first, last = group
    rows = v_ref.shape[0]
    parts = [slice(at, at + rows // 2) for at in (0, rows // 2)]
    work = [(h, part) for h in range(first, last) for part in parts]

    def product(h, part):
        low, high = window(h)
        return nn(v_ref[part, low:high], embed(gt_ref[head_rows(h), :], h))

    following = product(*work[0])
    for index, (h, part) in enumerate(work):
        grad_prob = following
        if index + 1 < len(work):
            following = product(*work[index + 1])
        at, head = h - first, head_rows(h)
        here = head_rows(at)
        prob = p_ref[at, part, :].astype(F32) * factor_ref[h : h + 1, :]
        dv_ref[here, part] = nt(gt_ref[head, :], prob.astype(BF16))
        dscore = (prob * (grad_prob - delta_ref[h : h + 1, :])).astype(BF16)
        dk_ref[here, part] = nt(qt_ref[head, :], dscore)
        term = nn(kt_ref[head, part], dscore)
        dqt = term + (dq2_ref[head, :] if part is parts[0] else dqt)
        if part is parts[1]:
            dqt_ref[here, :] = (dqt * SCALE).astype(BF16)


def backward_kernel(group, *refs):
    backward_heads(group, *refs[:8], *refs[9:])


def turning_backward_kernel(group, *refs):
    ot_ref, out_ref = refs[9:11]
    backward_heads(group, *refs[:8], *refs[11:])
    out_ref[...] = ot_ref[...].T


def last_backward_kernel(groups, index, *refs):
    others = len(groups) - 1
    lanes_ref, back_ref, out_ref, after_ref = refs[8:12]
    terms = refs[12 : 12 + 3 * others]
    out_any, dq_any, sum_ref, dqt_ref, dk_ref, dv_ref, turned_ref, wide_ref, dq_ref, sems = refs[12 + 3 * others :]
    copies = [
        pltpu.make_async_copy(out_ref, out_any, sems.at[0]),
        pltpu.make_async_copy(dq_ref, dq_any, sems.at[1]),
    ]
    copies[0].start()
    backward_heads(groups[index], *refs[:8], dqt_ref, dk_ref, dv_ref)

    def all_groups(at, mine):
        found = list(terms[at * others : (at + 1) * others])
        found.insert(index, mine)
        return found

    rows, width = dq_ref.shape
    near_rows = rows // CENTER_DILATION
    for (first, last), ref in zip(groups, all_groups(0, dqt_ref)):
        turned_ref[first * HEAD_WIDTH : last * HEAD_WIDTH, :] = ref[...]
    dq_ref[...] = turned_ref[...].T
    copies[1].start()
    for at, parts, by in ((0, all_groups(1, dk_ref), SCALE), (width, all_groups(2, dv_ref), 1.0)):
        for (first, last), ref in zip(groups, parts):
            wide_ref[first * HEAD_WIDTH : last * HEAD_WIDTH, :] = ref[...] * by
        for low in range(0, width, LANES):
            block = (at + low) // LANES
            sum_ref[block] = wide_ref[low : low + LANES, :].T
            near = back_ref[:, at + low : at + low + LANES].astype(F32)
            center = lanes_ref[0:1, low : low + LANES]
            for step in range(CENTER_DILATION):
                strided = pl.ds(step, near_rows, stride=CENTER_DILATION)
                sum_ref[block, strided, :] += jnp.where(center == step, near, 0.0)
    for copy in copies:
        copy.wait()


def combine_kernel(lanes_ref, sum_ref, far_ref, outk_ref, outv_ref):
    rows, width = outk_ref.shape
    far_rows = far_ref.shape[0]
    row = lax.broadcasted_iota(jnp.int32, (WIDE_DILATION, LANES), 0)
    for at, out in ((0, outk_ref), (width, outv_ref)):
        for low in range(0, width, LANES):
            block = (at + low) // LANES
            mask = row == lanes_ref[1:2, low : low + LANES]
            for index in range(far_rows):
                part = slice(index * WIDE_DILATION, (index + 1) * WIDE_DILATION)
                far = far_ref[index : index + 1, at + low : at + low + LANES]
                value = sum_ref[block, part, :] + jnp.where(mask, far, 0.0)
                out[part, low : low + LANES] = value.astype(BF16)


ANY = pl.BlockSpec(memory_space=pl.ANY)
HBM = pl.BlockSpec(memory_space=pltpu.HBM)


def call(body, outs, ins, scratch=(), *, in_hbm=0, flops=0, moved=0):
    return pl.pallas_call(
        body,
        out_shape=[jax.ShapeDtypeStruct(s, d) for s, d in outs],
        in_specs=ins,
        out_specs=[HBM] * in_hbm + [VMEM] * (len(outs) - in_hbm),
        scratch_shapes=list(scratch),
        compiler_params=pltpu.CompilerParams(vmem_limit_bytes=24 * 2**20),
        cost_estimate=pl.CostEstimate(flops=flops, bytes_accessed=moved, transcendentals=0),
    )


def local(queries, keys, values, grad_out, center_shift, wide_shift, valid_count):
    rows, width = queries.shape
    heads = width // HEAD_WIDTH
    groups = head_groups(heads)
    near_rows, far_own = rows // CENTER_DILATION, rows // WIDE_DILATION
    axes = ("seq", "sub")
    devices = lax.axis_size(axes)
    far_rows = far_own * devices
    blocks = 2 * width // LANES
    steps = [2**bit for bit in range(devices.bit_length() - 1)]

    def swap(value, apart):
        return lax.ppermute(value, axes, [(at, at ^ apart) for at in range(devices)])

    far, q, k, v, table, lanes = call(
        functools.partial(select_kernel, heads),
        [((far_own, 2 * width), BF16)]
        + [((rows, width), BF16)] * 3
        + [((2 * heads, rows), jnp.int32), ((8, width), jnp.int32)],
        [HBM] * 5,
        [
            pltpu.SMEM(center_shift.shape, jnp.int32),
            pltpu.SMEM(wide_shift.shape, jnp.int32),
            pltpu.SemaphoreType.DMA((5,)),
        ],
        moved=16 * rows * width,
    )(
        *(
            pltpu.with_memory_space_constraint(value, pltpu.HBM)
            for value in (center_shift, wide_shift, queries, keys, values)
        )
    )

    valid, far = lax.optimization_barrier((valid_count, far))

    def cost(heads_done, keys_done, products):
        done = heads_done * keys_done * rows
        return dict(flops=2 * HEAD_WIDTH * done * products * 5, moved=2 * done)

    turned = {}
    fronts = {}

    def front(index, after):
        first, last = groups[index]
        size, tall = last - first, (last - first) * HEAD_WIDTH
        outs = [((size, rows, rows), BF16), ((tall, rows), F32), ((size, rows), F32), ((size, rows), F32)]
        if not turned:
            *flipped, p, o, top, total = call(
                functools.partial(first_forward_kernel, groups[index], heads),
                [((near_rows, 2 * width), BF16)] + [((width, rows), BF16)] * 2 + outs,
                [SMEM] + [VMEM] * 5 + [ANY],
                [pltpu.VMEM((2, blocks // 2, rows, LANES), F32)],
                **cost(size, rows, 2),
            )(valid, table, k, q, v, lanes, after)
            turned.update(zip(("near", "qt", "vt"), flipped))
        else:
            p, o, top, total = call(
                functools.partial(forward_kernel, groups[index], heads),
                outs,
                [SMEM] + [VMEM] * 4 + [ANY],
                **cost(size, rows, 2),
            )(valid, table, k, turned["qt"], turned["vt"], after)
        fronts[index] = [p, o, top, total]

    def tie(arrived, holder, key):
        arrived, held = lax.optimization_barrier((arrived, holder[key][-1]))
        holder[key] = [*holder[key][:-1], held]
        return arrived

    last = len(groups) - 1
    front_order, back_order = [last, *range(last)], [*range(last, -1, -1)]
    after = far
    for at, step in enumerate(steps):
        if at == 1:
            near_out, far = lax.optimization_barrier((turned["near"], far))
        arrived = swap(far, step)
        if at == 1:
            near_came = swap(near_out, 1)
        if at < len(groups):
            front(front_order[at], after)
        if at == len(groups) - 1:
            p, o, top, total = zip(*(fronts[index] for index in range(len(groups))))
            fronts["near"] = call(
                functools.partial(near_forward_kernel, heads, groups),
                [((width, rows), BF16)] * 2
                + [((heads * near_rows, rows), BF16), ((width, rows), F32)]
                + [((heads, rows), F32)] * 3,
                [SMEM] + [VMEM] * (5 + 3 * len(groups)) + [ANY],
                **cost(heads, near_rows, 2),
            )(valid, table, near_came, turned["qt"], k, grad_out, *o, *top, *total, after)
            arrived = tie(arrived, fronts, "near")
        elif at < len(groups):
            arrived = tie(arrived, fronts, front_order[at])
        after = arrived
        far = jnp.concatenate([far, arrived], axis=0)
    gt, kt, near_p, o, old, near_top, near_sum = fronts["near"]
    qt = turned["qt"]

    ot, local_factor, near_factor, delta, ds, terms, send = call(
        functools.partial(wide_kernel, heads, far_own),
        [((width, rows), BF16)]
        + [((heads, rows), F32)] * 3
        + [((heads * far_rows, rows), BF16)]
        + [((far_rows // 2, 2 * width), F32), ((far_rows // 2, 2 * width), BF16)],
        [SMEM] + [VMEM] * 8,
        [pltpu.VMEM((far_rows, 2 * width), F32)],
        **cost(heads, far_rows, 5),
    )(valid, table, far, qt, gt, o, old, near_top, near_sum)

    backs = {}

    def back(index, after):
        first, end = groups[index]
        size, tall = end - first, (end - first) * HEAD_WIDTH
        partial = [((tall, rows), BF16), ((tall, rows), F32), ((tall, rows), F32)]
        given = (p[index], qt, gt, kt, v, backs["near"][0], local_factor, delta)
        if len(backs) == OUT_AT:
            backs["out"], *backs[index] = call(
                functools.partial(turning_backward_kernel, groups[index]),
                [((rows, width), BF16), *partial],
                [VMEM] * 8 + [ANY, VMEM],
                **cost(size, rows, 4),
            )(*given, after, ot)
            return
        if len(backs) < len(groups):
            backs[index] = call(
                functools.partial(backward_kernel, groups[index]),
                partial,
                [VMEM] * 8 + [ANY],
                **cost(size, rows, 4),
            )(*given, after)
            return
        others = [backs[other] for other in range(len(groups)) if other != index]
        backs["out"], *backs[index] = call(
            functools.partial(last_backward_kernel, groups, index),
            [((rows, width), BF16)] * 2 + [((blocks, rows, LANES), F32)],
            [VMEM] * 11 + [ANY] + [VMEM] * (3 * len(others)),
            [pltpu.VMEM(shape, dtype) for shape, dtype in partial]
            + [pltpu.VMEM((width, rows), BF16), pltpu.VMEM((width, rows), F32)]
            + [pltpu.VMEM((rows, width), BF16), pltpu.SemaphoreType.DMA((2,))],
            in_hbm=2,
            **cost(size, rows, 4),
        )(*given, lanes, near_back, backs["out"], after, *[terms[i] for i in range(3) for terms in others])

    after = send
    for at, step in enumerate(reversed(steps)):
        if at:
            half = terms.shape[0] // 2
            send, terms = terms[half:], terms[:half]
        arrived = swap(send, step)
        if at == 0:
            backs["near"] = call(
                functools.partial(near_backward_kernel, heads),
                [((width, rows), F32), ((near_rows, 2 * width), BF16)],
                [VMEM] * 8 + [ANY],
                [pltpu.VMEM((near_rows, 2 * width), F32)],
                **cost(heads, near_rows, 4),
            )(near_came, far, qt, gt, near_p, ds, near_factor, delta, after)
        if at == 1:
            near_back = swap(backs["near"][1], 1)
        if at < len(groups):
            back(back_order[at], after)
            arrived = tie(arrived, backs, back_order[at])
        after = arrived
        terms = terms + arrived.astype(F32)

    dq, sums = backs[back_order[-1]]
    key_gradient, value_gradient = call(
        combine_kernel,
        [((rows, width), BF16)] * 2,
        [VMEM] * 3,
        moved=12 * rows * width,
    )(lanes, sums, terms)
    return backs["out"], dq, key_gradient, value_gradient


def solution(mesh):
    split = P(("grp", "seq", "sub"), "hd")
    return jax.shard_map(
        local,
        mesh=mesh,
        in_specs=(split, split, split, split, P(), P(), P("grp")),
        out_specs=(split, split, split, split),
        check_vma=False,
    )
```
